512 devices in a mesh: event: 16 (over z_lo, x), mesh: 32 (over y, z_hi, core).
Axes of the slice: x: 4, y: 4, z: 16 (z_hi: 4, z_lo: 4; z = z_hi * 4 + z_lo), core: 2. Of those that a mesh axis runs over, the one named last changes fastest.
Arguments:
- kernels: float32 [32, 6, 32768], P('event', None, 'mesh'), may hold values from -4 to 4
- basis: float32 [256, 4, 128, 128], P('mesh'), may hold values from -1.25 to 1.25
- support_index: int32 [256, 4], P('mesh'), may hold values from -1 to 127, as said below
- owner_order: int32 [128], replicated, may hold values from 0 to 127, each once
- precond: float32 [128, 6, 128], P('mesh'), may hold values from 0.5 to 4
- damping: float32 [6], replicated, may hold values from 0.2 to 2
Outputs:
- model_update: float32 [6, 32768], P(None, 'mesh')
- update: float32 [128, 6, 128], P('mesh')
The draws below stay inside these ranges and needn't reach their ends.
Inputs may be any that keep to these rules, and one draw needn't show every extreme that they name: `support_index`: the blocks of the slots of one tile are distinct; padded slots hold -1 and only the last slot of a tile may be padded.
All inputs are finite; a program needn't handle non-finite values.
Results may differ from the reference program's by a relative error of at most 0.000073.
Values sent between devices are 32-bit elements; how exact they have to be, the bound alone decides.
A program may use at most 64 MiB of HBM per device.

```python
import math
import jax
import jax.numpy as jnp
from jax import lax

P_SIZE = 6
CB = 128
TILE = 128
SUP = 4
NTILES = 256
PTS = 32768
NBLK = 128
EVENTS = 32


def draw_support_index(key, part):
    key = jax.random.fold_in(key, 5)
    first_key, second_key, third_key = jax.random.split(key, 3)
    tile_ids = jnp.arange(NTILES, dtype=jnp.int32)
    start_block = jax.random.randint(first_key, (NTILES,), 0, NBLK)
    start_block = jnp.where(tile_ids == 0, NBLK - 1, start_block)
    widest_gap = max(1, (NBLK - 1) // (SUP - 1))
    slot_ids = jnp.arange(SUP, dtype=jnp.int32)
    increments = jax.random.randint(second_key, (NTILES, SUP), 1, widest_gap + 1)
    increments = jnp.where(slot_ids[None, :] == 0, 0, increments)
    offsets = jnp.cumsum(increments, axis=1)
    block_ids = (start_block[:, None] + offsets) % NBLK
    padded = jax.random.randint(third_key, (NTILES,), 0, 2) == 1
    padded = jnp.logical_or(padded, tile_ids == 0)
    last_slot = slot_ids[None, :] == SUP - 1
    block_ids = jnp.where(jnp.logical_and(last_slot, padded[:, None]), -1, block_ids)
    return block_ids.astype(jnp.int32)


def levels(stream_key, shape, pieces, smallest, top_value):
    def one(axis_at, shards_of):
        heights = jax.random.uniform(jax.random.fold_in(jax.random.fold_in(stream_key, 6), axis_at), (shards_of,), jnp.float32, smallest / len(pieces), top_value / len(pieces))
        return jnp.repeat(jnp.exp(heights), shape[axis_at] // shards_of).reshape((-1,) + (1,) * (len(shape) - axis_at - 1))

    level = one(*pieces[0])
    for cut in pieces[1:]:
        level = level * one(*cut)
    return level


def bell_draw(stream_key, extent, width, bound, cuts=(), kind=jnp.bfloat16):
    level = levels(stream_key, extent, cuts, -0.22, 0.18) if cuts else 1.0
    array = jax.random.normal(stream_key, extent, jnp.float32) * width * level
    return jnp.minimum(jnp.maximum(array, -bound), bound).astype(kind)


def setup_inputs(seed: int = 0) -> dict:
    keys = jax.random.split(jax.random.key(seed), 7)
    kernels = bell_draw(keys[0], (EVENTS, P_SIZE, PTS), 0.25, 4.0, ((0, 16), (2, 32)), jnp.float32)
    basis = bell_draw(keys[1], (NTILES, SUP, CB, TILE), (TILE ** -0.5), 1.25, ((0, 32),), jnp.float32)
    support_index = draw_support_index(jax.random.fold_in(keys[6], 71), 0)
    owner_order = jax.random.permutation(keys[3], NBLK).astype(jnp.int32)
    precond = jnp.clip(jnp.exp(math.log(4.0) - 2.0794415 * jax.random.uniform(keys[4], (NBLK, P_SIZE, CB), jnp.float32) ** levels(keys[4], (NBLK, P_SIZE, CB), ((0, 32),), -0.2, 0.2)), 0.5, 4.0)
    damping = jnp.clip(jnp.exp(jax.random.uniform(keys[5], (P_SIZE,), jnp.float32, math.log(0.2), math.log(2.0))), 0.2, 2.0)
    return {"kernels": kernels, "basis": basis, "support_index": support_index, "owner_order": owner_order, "precond": precond, "damping": damping}


def reference(kernels, basis, support_index, owner_order, precond, damping):
    precise = lax.Precision.HIGHEST
    summed = jnp.sum(kernels, axis=0)
    tile_grid = summed.reshape(P_SIZE, NTILES, TILE)
    projected = jnp.einsum('tscx,ptx->tspc', basis, tile_grid, precision=precise)
    flattened = projected.reshape(NTILES * SUP, P_SIZE * CB)
    slot_ids = support_index.reshape(-1)
    selector = (slot_ids[:, None] == owner_order[None, :]).astype(jnp.float32)
    owned = jnp.einsum('kj,kf->jf', selector, flattened, precision=precise)
    update = -owned.reshape(NBLK, P_SIZE, CB) / (damping[None, :, None] + precond)
    picked = jnp.einsum('kj,jf->kf', selector, update.reshape(NBLK, P_SIZE * CB), precision=precise)
    picked = picked.reshape(NTILES, SUP, P_SIZE, CB)
    model_update = jnp.einsum('tscx,tspc->ptx', basis, picked, precision=precise).reshape(P_SIZE, PTS)
    return model_update, update
```

```python
import jax
import jax.numpy as jnp
from jax import lax
from jax.experimental import pallas as pl
from jax.experimental.pallas import tpu as pltpu
from jax.sharding import PartitionSpec as P

MESH = pl.DeviceIdType.MESH
F32 = jnp.float32
BF16 = jnp.bfloat16
TILES = 8
SLOTS = 4
PN = 6
NT = (((1,), (1,)), ((), ()))
NN = (((1,), (0,)), ((), ()))


def split3(v):
    hi = v.astype(BF16)
    rest = v - hi.astype(F32)
    mid = rest.astype(BF16)
    low = (rest - mid.astype(F32)).astype(BF16)
    return hi, mid, low


def iota(shape, dim):
    return lax.broadcasted_iota(jnp.int32, shape, dim)


def fold3(v):
    n = v.shape[0] // 3
    return v[0:n] + v[n : 2 * n] + v[2 * n : 3 * n]


def kernel(
    kern_hbm, basis_hbm, sup_hbm, own_hbm, pre_hbm, damp_hbm,
    model_ref, upd_ref,
    kern_v, basis_v, own_v, pre_v, sup_s, damp_s,
    halves, proj, src1, buf1, buf2, src3, buf3, turned,
    left, weight1, weight3, weight2, key,
    load_sem, tile_sem, send_sem, recv_sem, self_sem,
):
    ev = lax.axis_index("event")
    me = lax.axis_index("mesh")
    x, z0, z1 = lax.rem(ev, 4), lax.rem(lax.div(ev, 4), 2), lax.div(ev, 8)
    core, zh, y = lax.rem(me, 2), lax.rem(lax.div(me, 2), 4), lax.div(me, 8)

    def device(x_, z0_, z1_, core_, zh_, y_):
        return (z1_ * 8 + z0_ * 4 + x_, y_ * 8 + zh_ * 2 + core_)

    xs = [x] + [lax.rem(x + d, 4) for d in (1, 2, 3)]
    ys = [y] + [lax.rem(y + d, 4) for d in (1, 2, 3)]
    cs = [core, 1 - core]
    z0s = [z0, 1 - z0]
    z1s = [z1, 1 - z1]
    zhs = [zh] + [lax.rem(zh + d, 4) for d in (1, 2, 3)]
    slab = y * 2 + core
    mine = slab * 8 + z0 * 4 + x
    far = zh * 2 + z1

    local_peers = []
    for dy in (2, 1, 3, 0):
        for dx in (2, 1, 3, 0):
            for dz in (1, 0):
                for dc in (1, 0):
                    if dy or dx or dz or dc:
                        s = ys[dy] * 2 + cs[dc]
                        i = s * 8 + z0s[dz] * 4 + xs[dx]
                        local_peers.append((device(xs[dx], z0s[dz], z1, cs[dc], zh, ys[dy]), s, i))
    far_peers = [
        device(x, z0, z1s[b], core, zhs[a], y) for a in (2, 1, 3, 0) for b in (1, 0) if a or b
    ]

    barrier = pltpu.get_barrier_semaphore()
    for peer in [p[0] for p in local_peers] + far_peers:
        pl.semaphore_signal(barrier, inc=1, device_id=peer, device_id_type=MESH)

    loads = [
        pltpu.make_async_copy(a, b, load_sem.at[n])
        for n, (a, b) in enumerate(
            ((kern_hbm, kern_v), (pre_hbm, pre_v), (own_hbm, own_v), (sup_hbm, sup_s), (damp_hbm, damp_s))
        )
    ]
    tiles = [pltpu.make_async_copy(basis_hbm.at[t], basis_v.at[t], tile_sem.at[t]) for t in range(TILES)]
    for c in loads:
        c.start()
    for c in tiles:
        c.start()

    row8, lane8 = iota((8, 128), 0), iota((8, 128), 1)
    in8, group = lax.rem(lane8, 8), lax.div(lane8, 8)
    one = lambda c: jnp.where(c, 1.0, 0.0).astype(F32)
    data = (in8 == row8) & (row8 < PN)
    mask1 = [
        one(data | ((in8 == PN) & (row8 == 6))),
        one(data | ((in8 == PN) & (row8 == 7) & (group < 8))),
    ]
    mask3 = [
        one(data | ((in8 == PN) & (lax.div(group, 4) == row8))),
        one(data | ((in8 == PN) & (lax.div(group, 4) + 4 == row8) & (group < 8))),
    ]
    mask2 = one((lax.div(lane8, 32) == lax.rem(row8, 4)) & (row8 < PN))

    nrow, nlane = iota((128, 128), 0), iota((128, 128), 1)
    for a in range(4):
        target = lax.div(lax.rem(nlane, 32), 8) * 32 + a * 8 + lax.rem(nlane, 8)
        weight2[:, a * 128 : (a + 1) * 128] = one(nrow == target).astype(BF16)

    loads[0].wait()
    summed = kern_v[0] + kern_v[1]
    summed = jnp.concatenate([summed, jnp.zeros((2, summed.shape[1]), F32)], axis=0)
    terms = jnp.concatenate([*split3(summed), jnp.zeros(summed.shape, BF16)], axis=0)

    for t in range(TILES):
        tiles[t].wait()
        part = basis_v[t].reshape(SLOTS * 128, 128)
        hi = part.astype(BF16)
        low = (part - hi.astype(F32)).astype(BF16)
        both = jnp.concatenate([hi, low], axis=1)
        halves[t] = both
        here = terms[:, t * 128 : (t + 1) * 128]
        got = lax.dot_general(jnp.concatenate([here, here], axis=1), both, NT, preferred_element_type=F32)
        got = got[0:8] + got[8:16] + got[16:24]
        for s in range(SLOTS):
            proj[(t * SLOTS + s) * 8 : (t * SLOTS + s + 1) * 8, :] = got[:, s * 128 : (s + 1) * 128]

    for c in loads[1:]:
        c.wait()
    prow = iota((PN, 128), 0)
    damp = jnp.zeros((PN, 128), F32)
    for p in range(PN):
        damp = jnp.where(prow == p, damp_s[p], damp)
    for j in range(4):
        proj[pl.ds(6 + 8 * j, PN, stride=32), :] = -0.125 / (damp + pre_v[j])
    for t in range(TILES):
        for s in range(SLOTS):
            r = (t * SLOTS + s) * 8 + 7
            proj[r : r + 1, :] = jnp.full((1, 128), sup_s[t, s].astype(F32) * 0.125)

    for h in range(2):
        turn = proj[h * 128 : (h + 1) * 128, :].T
        for c in range(2):
            src1[pl.ds(c * 2 + h, 64, stride=4), :] = turn[c * 64 : (c + 1) * 64]

    owner = jnp.broadcast_to(own_v[...].astype(F32), (128, 128)).T
    key[...] = jnp.where(lax.rem(nlane, 8) == PN, nrow.astype(F32), owner)

    pl.semaphore_wait(barrier, len(local_peers) + len(far_peers))

    def rows(ref, i):
        return ref.at[pl.ds(pl.multiple_of(i * 4, 4), 4), :]

    def exchange(phase, src, dst, pick):
        for dev, s, i in local_peers:
            pltpu.make_async_remote_copy(
                src_ref=rows(src, pick(s, i)),
                dst_ref=rows(dst, mine),
                send_sem=send_sem.at[phase],
                recv_sem=recv_sem.at[phase],
                device_id=dev,
                device_id_type=MESH,
            ).start()
        own = pltpu.make_async_copy(rows(src, pick(slab, mine)), rows(dst, mine), self_sem.at[phase])
        own.start()
        count = 4 * len(local_peers)
        whole = pltpu.make_async_remote_copy(
            src_ref=dst.at[pl.ds(0, count), :],
            dst_ref=dst.at[pl.ds(0, count), :],
            send_sem=send_sem.at[phase],
            recv_sem=recv_sem.at[phase],
            device_id=local_peers[0][0],
            device_id_type=MESH,
        )
        return own, whole

    own1, whole1 = exchange(0, src1, buf1, lambda s, i: i)

    low_lane = iota((1, 128), 1)
    low_in8, low_group = lax.rem(low_lane, 8), lax.div(low_lane, 8)

    own1.wait()
    whole1.wait_recv()
    ids = []
    for s in range(8):
        v = buf1[s * 32 : s * 32 + 8] + buf1[s * 32 + 8 : s * 32 + 16]
        v = v + (buf1[s * 32 + 16 : s * 32 + 24] + buf1[s * 32 + 24 : s * 32 + 32])
        v = v + pltpu.roll(v, 4, 0)
        name = jnp.where(in8 == 7, v, 0.0)
        for d in (1, 2, 4):
            name = name + pltpu.roll(name, 128 - d, 1)
        ids.append(name)
        for h in range(2):
            at = slice((s * 2 + h) * 128, (s * 2 + h + 1) * 128)
            both = jnp.concatenate(
                [jnp.broadcast_to(v[c * 2 + h : c * 2 + h + 1], (8, 128)) * mask1[h] for c in range(2)], axis=0
            )
            left[:, at] = jnp.concatenate(split3(both), axis=0)
            slot = low_group + 16 * h
            code = lax.rem(lax.div(slot, 4), 4) * 32 + s * 4 + lax.rem(slot, 4)
            code = jnp.where(slot < 24, code, -1).astype(F32)
            code = jnp.where(low_in8 == PN, code, name[h : h + 1])
            weight1[:, at] = one(key[...] == code).astype(BF16)
    dense = fold3(lax.dot_general(left[...], weight1[...], NT, preferred_element_type=F32))
    buf2[far] = dense
    for n, dev in enumerate(far_peers):
        pltpu.make_async_remote_copy(
            src_ref=buf2.at[far],
            dst_ref=buf2.at[far],
            send_sem=send_sem.at[1],
            recv_sem=recv_sem.at[1],
            device_id=dev,
            device_id_type=MESH,
        ).start()

    for s in range(8):
        block = (s // 2 * 8 + zh * 2 + s % 2) * 4
        for h in range(2):
            slot = low_group + 16 * h
            code = jnp.where(slot < 24, block + lax.rem(slot, 4), -1).astype(F32)
            code = jnp.where(low_in8 == PN, code, ids[s][h : h + 1])
            weight3[:, (s * 2 + h) * 128 : (s * 2 + h + 1) * 128] = one(key[...] == code).astype(BF16)

    whole2 = pltpu.make_async_remote_copy(
        src_ref=buf2.at[pl.ds(0, 7)],
        dst_ref=buf2.at[pl.ds(0, 7)],
        send_sem=send_sem.at[1],
        recv_sem=recv_sem.at[1],
        device_id=far_peers[0],
        device_id_type=MESH,
    )
    whole2.wait_recv()
    spread = []
    for a in range(4):
        v = buf2[a * 2]
        spread.append(
            jnp.concatenate(
                [
                    jnp.where(
                        row8 < 4,
                        jnp.broadcast_to(v[c * 8 + 6 : c * 8 + 7], (8, 128)),
                        jnp.broadcast_to(v[c * 8 + 7 : c * 8 + 8], (8, 128)),
                    )
                    * mask2
                    for c in range(2)
                ],
                axis=0,
            )
        )
    spread = jnp.concatenate(split3(jnp.concatenate(spread, axis=1)), axis=0)
    factor = fold3(lax.dot_general(spread, weight2[...], NT, preferred_element_type=F32))
    total = buf2[0]
    for f in range(1, 8):
        total = total + buf2[f]
    update = jnp.concatenate(split3(total * factor), axis=0)
    picked = fold3(lax.dot_general(update, weight3[...], NN, preferred_element_type=F32))
    for s in range(8):
        for h in range(2):
            for c in range(2):
                v = picked[c * 8 : c * 8 + 8, (s * 2 + h) * 128 : (s * 2 + h + 1) * 128] * mask3[h]
                r = s * 4 + c * 2 + h
                src3[r : r + 1, :] = jnp.sum(v, axis=0, keepdims=True)

    own3, whole3 = exchange(2, src3, buf3, lambda s, i: s)
    own3.wait()
    whole3.wait_recv()
    for h in range(2):
        block = jnp.concatenate([buf3[pl.ds(c * 2 + h, 64, stride=4), :] for c in range(2)], axis=0)
        turned[h * 128 : (h + 1) * 128, :] = block.T
    for t in range(TILES):
        lhs = jnp.concatenate(
            [turned[(t * SLOTS + s) * 8 : (t * SLOTS + s + 1) * 8, :] for s in range(SLOTS)], axis=1
        )
        lhs = jnp.concatenate([*split3(lhs), jnp.zeros(lhs.shape, BF16)], axis=0)
        got = lax.dot_general(lhs, halves[t], NN, preferred_element_type=F32)
        got = got[0:8] + got[8:16] + got[16:24]
        got = got[:, 0:128] + got[:, 128:256]
        model_ref[:, t * 128 : (t + 1) * 128] = got[0:PN]
    for j in range(4):
        upd_ref[j] = turned[pl.ds(6 + 8 * j, PN, stride=32), :]
    whole1.wait_send()
    whole2.wait_send()
    whole3.wait_send()


def local(kernels, basis, support_index, owner_order, precond, damping):
    hbm = pl.BlockSpec(memory_space=pl.ANY)
    vmem = pl.BlockSpec(memory_space=pltpu.VMEM)
    points = TILES * 128
    return pl.pallas_call(
        kernel,
        out_shape=(
            jax.ShapeDtypeStruct((PN, points), F32),
            jax.ShapeDtypeStruct((4, PN, 128), F32),
        ),
        in_specs=[hbm] * 6,
        out_specs=(vmem, vmem),
        scratch_shapes=[
            pltpu.VMEM((2, PN, points), F32),
            pltpu.VMEM((TILES, SLOTS, 128, 128), F32),
            pltpu.VMEM((1, 128), jnp.int32),
            pltpu.VMEM((4, PN, 128), F32),
            pltpu.SMEM((TILES, SLOTS), jnp.int32),
            pltpu.SMEM((PN,), F32),
            pltpu.VMEM((TILES, SLOTS * 128, 256), BF16),
            pltpu.VMEM((256, 128), F32),
            pltpu.VMEM((256, 128), F32),
            pltpu.VMEM((256, 128), F32),
            pltpu.VMEM((8, 16, 128), F32),
            pltpu.VMEM((32, 128), F32),
            pltpu.VMEM((256, 128), F32),
            pltpu.VMEM((256, 128), F32),
            pltpu.VMEM((48, 2048), BF16),
            pltpu.VMEM((128, 2048), BF16),
            pltpu.VMEM((128, 2048), BF16),
            pltpu.VMEM((128, 512), BF16),
            pltpu.VMEM((128, 128), F32),
            pltpu.SemaphoreType.DMA((5,)),
            pltpu.SemaphoreType.DMA((TILES,)),
            pltpu.SemaphoreType.DMA((3,)),
            pltpu.SemaphoreType.DMA((3,)),
            pltpu.SemaphoreType.DMA((3,)),
        ],
        compiler_params=pltpu.CompilerParams(
            collective_id=0, has_side_effects=True, vmem_limit_bytes=40 * 1024 * 1024
        ),
        cost_estimate=pl.CostEstimate(flops=10**9, bytes_accessed=2 * 10**6, transcendentals=0),
    )(kernels, basis, support_index, owner_order.reshape(1, 128), precond, damping)


def solution(mesh):
    in_specs = (
        P("event", None, "mesh"),
        P("mesh", None, None, None),
        P("mesh", None),
        P(),
        P("mesh", None, None),
        P(),
    )
    out_specs = (P(None, "mesh"), P("mesh", None, None))
    return jax.shard_map(local, mesh=mesh, in_specs=in_specs, out_specs=out_specs, check_vma=False)
```

```python
import jax
import jax.numpy as jnp
from jax import lax
from jax.experimental import pallas as pl
from jax.experimental.pallas import tpu as pltpu
from jax.sharding import PartitionSpec as P

MESH = pl.DeviceIdType.MESH
F32 = jnp.float32
BF16 = jnp.bfloat16
TILES = 8
SLOTS = 4
PN = 6
NT = (((1,), (1,)), ((), ()))
NN = (((1,), (0,)), ((), ()))


def split3(v):
    hi = v.astype(BF16)
    rest = v - hi.astype(F32)
    mid = rest.astype(BF16)
    low = (rest - mid.astype(F32)).astype(BF16)
    return hi, mid, low


def iota(shape, dim):
    return lax.broadcasted_iota(jnp.int32, shape, dim)


def fold3(v):
    n = v.shape[0] // 3
    return v[0:n] + v[n : 2 * n] + v[2 * n : 3 * n]


def kernel(
    kern_hbm, basis_hbm, sup_hbm, own_hbm, pre_hbm, damp_hbm,
    model_ref, upd_ref,
    kern_v, basis_v, own_v, pre_v, sup_s, damp_s,
    halves, proj, src1, buf1, buf2, src3, buf3, turned,
    left, weight1, weight3, weight2, key,
    load_sem, tile_sem, send_sem, recv_sem, self_sem,
):
    ev = lax.axis_index("event")
    me = lax.axis_index("mesh")
    x, z0, z1 = lax.rem(ev, 4), lax.rem(lax.div(ev, 4), 2), lax.div(ev, 8)
    core, zh, y = lax.rem(me, 2), lax.rem(lax.div(me, 2), 4), lax.div(me, 8)

    def device(x_, z0_, z1_, core_, zh_, y_):
        return (z1_ * 8 + z0_ * 4 + x_, y_ * 8 + zh_ * 2 + core_)

    xs = [x] + [lax.rem(x + d, 4) for d in (1, 2, 3)]
    ys = [y] + [lax.rem(y + d, 4) for d in (1, 2, 3)]
    cs = [core, 1 - core]
    z0s = [z0, 1 - z0]
    z1s = [z1, 1 - z1]
    zhs = [zh] + [lax.rem(zh + d, 4) for d in (1, 2, 3)]
    slab = y * 2 + core
    mine = slab * 8 + z0 * 4 + x
    far = zh * 2 + z1

    local_peers = []
    for dy in (2, 1, 3, 0):
        for dx in (2, 1, 3, 0):
            for dz in (1, 0):
                for dc in (1, 0):
                    if dy or dx or dz or dc:
                        s = ys[dy] * 2 + cs[dc]
                        i = s * 8 + z0s[dz] * 4 + xs[dx]
                        local_peers.append((device(xs[dx], z0s[dz], z1, cs[dc], zh, ys[dy]), s, i))
    far_peers = [
        device(x, z0, z1s[b], core, zhs[a], y) for a in (2, 1, 3, 0) for b in (1, 0) if a or b
    ]

    barrier = pltpu.get_barrier_semaphore()
    for peer in [p[0] for p in local_peers] + far_peers:
        pl.semaphore_signal(barrier, inc=1, device_id=peer, device_id_type=MESH)

    loads = [
        pltpu.make_async_copy(a, b, load_sem.at[n])
        for n, (a, b) in enumerate(
            ((kern_hbm, kern_v), (pre_hbm, pre_v), (own_hbm, own_v), (sup_hbm, sup_s), (damp_hbm, damp_s))
        )
    ]
    tiles = [pltpu.make_async_copy(basis_hbm.at[t], basis_v.at[t], tile_sem.at[t]) for t in range(TILES)]
    for c in loads:
        c.start()
    for c in tiles:
        c.start()

    row8, lane8 = iota((8, 128), 0), iota((8, 128), 1)
    in8, group = lax.rem(lane8, 8), lax.div(lane8, 8)
    one = lambda c: jnp.where(c, 1.0, 0.0).astype(F32)
    data = (in8 == row8) & (row8 < PN)
    mask1 = [
        one(data | ((in8 == PN) & (row8 == 6))),
        one(data | ((in8 == PN) & (row8 == 7) & (group < 8))),
    ]
    mask3 = [
        one(data | ((in8 == PN) & (lax.div(group, 4) == row8))),
        one(data | ((in8 == PN) & (lax.div(group, 4) + 4 == row8) & (group < 8))),
    ]
    mask2 = one((lax.div(lane8, 32) == lax.rem(row8, 4)) & (row8 < PN))

    nrow, nlane = iota((128, 128), 0), iota((128, 128), 1)
    for a in range(4):
        target = lax.div(lax.rem(nlane, 32), 8) * 32 + a * 8 + lax.rem(nlane, 8)
        weight2[:, a * 128 : (a + 1) * 128] = one(nrow == target).astype(BF16)

    loads[0].wait()
    summed = kern_v[:, 0, :] + kern_v[:, 1, :]
    summed = jnp.concatenate([summed, jnp.zeros((2, summed.shape[1]), F32)], axis=0)
    terms = jnp.concatenate([*split3(summed), jnp.zeros(summed.shape, BF16)], axis=0)

    for t in range(TILES):
        tiles[t].wait()
        part = basis_v[t].reshape(SLOTS * 128, 128)
        hi = part.astype(BF16)
        low = (part - hi.astype(F32)).astype(BF16)
        both = jnp.concatenate([hi, low], axis=1)
        halves[t] = both
        here = terms[:, t * 128 : (t + 1) * 128]
        got = lax.dot_general(jnp.concatenate([here, here], axis=1), both, NT, preferred_element_type=F32)
        got = got[0:8] + got[8:16] + got[16:24]
        for s in range(SLOTS):
            proj[(t * SLOTS + s) * 8 : (t * SLOTS + s + 1) * 8, :] = got[:, s * 128 : (s + 1) * 128]

    for c in loads[1:]:
        c.wait()
    prow = iota((PN, 128), 0)
    damp = jnp.zeros((PN, 128), F32)
    for p in range(PN):
        damp = jnp.where(prow == p, damp_s[p], damp)
    for j in range(4):
        proj[pl.ds(6 + 8 * j, PN, stride=32), :] = -0.125 / (damp + pre_v[:, j, :])
    for t in range(TILES):
        for s in range(SLOTS):
            r = (t * SLOTS + s) * 8 + 7
            proj[r : r + 1, :] = jnp.full((1, 128), sup_s[s, t].astype(F32) * 0.125)

    for h in range(2):
        turn = proj[h * 128 : (h + 1) * 128, :].T
        for c in range(2):
            src1[pl.ds(c * 2 + h, 64, stride=4), :] = turn[c * 64 : (c + 1) * 64]

    owner = jnp.broadcast_to(own_v[...].astype(F32), (128, 128)).T
    key[...] = jnp.where(lax.rem(nlane, 8) == PN, nrow.astype(F32), owner)

    pl.semaphore_wait(barrier, len(local_peers) + len(far_peers))

    def rows(ref, i):
        return ref.at[pl.ds(pl.multiple_of(i * 4, 4), 4), :]

    def exchange(phase, src, dst, pick):
        for dev, s, i in local_peers:
            pltpu.make_async_remote_copy(
                src_ref=rows(src, pick(s, i)),
                dst_ref=rows(dst, mine),
                send_sem=send_sem.at[phase],
                recv_sem=recv_sem.at[phase],
                device_id=dev,
                device_id_type=MESH,
            ).start()
        own = pltpu.make_async_copy(rows(src, pick(slab, mine)), rows(dst, mine), self_sem.at[phase])
        own.start()
        count = 4 * len(local_peers)
        whole = pltpu.make_async_remote_copy(
            src_ref=dst.at[pl.ds(0, count), :],
            dst_ref=dst.at[pl.ds(0, count), :],
            send_sem=send_sem.at[phase],
            recv_sem=recv_sem.at[phase],
            device_id=local_peers[0][0],
            device_id_type=MESH,
        )
        return own, whole

    own1, whole1 = exchange(0, src1, buf1, lambda s, i: i)

    low_lane = iota((1, 128), 1)
    low_in8, low_group = lax.rem(low_lane, 8), lax.div(low_lane, 8)

    own1.wait()
    whole1.wait_recv()
    ids = []
    for s in range(8):
        v = buf1[s * 32 : s * 32 + 8] + buf1[s * 32 + 8 : s * 32 + 16]
        v = v + (buf1[s * 32 + 16 : s * 32 + 24] + buf1[s * 32 + 24 : s * 32 + 32])
        v = v + pltpu.roll(v, 4, 0)
        name = jnp.where(in8 == 7, v, 0.0)
        for d in (1, 2, 4):
            name = name + pltpu.roll(name, 128 - d, 1)
        ids.append(name)
        for h in range(2):
            at = slice((s * 2 + h) * 128, (s * 2 + h + 1) * 128)
            both = jnp.concatenate(
                [jnp.broadcast_to(v[c * 2 + h : c * 2 + h + 1], (8, 128)) * mask1[h] for c in range(2)], axis=0
            )
            left[:, at] = jnp.concatenate(split3(both), axis=0)
            slot = low_group + 16 * h
            code = lax.rem(lax.div(slot, 4), 4) * 32 + s * 4 + lax.rem(slot, 4)
            code = jnp.where(slot < 24, code, -1).astype(F32)
            code = jnp.where(low_in8 == PN, code, name[h : h + 1])
            weight1[:, at] = one(key[...] == code).astype(BF16)
    dense = fold3(lax.dot_general(left[...], weight1[...], NT, preferred_element_type=F32))
    buf2[far] = dense
    for n, dev in enumerate(far_peers):
        pltpu.make_async_remote_copy(
            src_ref=buf2.at[far],
            dst_ref=buf2.at[far],
            send_sem=send_sem.at[1],
            recv_sem=recv_sem.at[1],
            device_id=dev,
            device_id_type=MESH,
        ).start()

    for s in range(8):
        block = (s // 2 * 8 + zh * 2 + s % 2) * 4
        for h in range(2):
            slot = low_group + 16 * h
            code = jnp.where(slot < 24, block + lax.rem(slot, 4), -1).astype(F32)
            code = jnp.where(low_in8 == PN, code, ids[s][h : h + 1])
            weight3[:, (s * 2 + h) * 128 : (s * 2 + h + 1) * 128] = one(key[...] == code).astype(BF16)

    whole2 = pltpu.make_async_remote_copy(
        src_ref=buf2.at[pl.ds(0, 7)],
        dst_ref=buf2.at[pl.ds(0, 7)],
        send_sem=send_sem.at[1],
        recv_sem=recv_sem.at[1],
        device_id=far_peers[0],
        device_id_type=MESH,
    )
    whole2.wait_recv()
    spread = []
    for a in range(4):
        v = buf2[a * 2]
        spread.append(
            jnp.concatenate(
                [
                    jnp.where(
                        row8 < 4,
                        jnp.broadcast_to(v[c * 8 + 6 : c * 8 + 7], (8, 128)),
                        jnp.broadcast_to(v[c * 8 + 7 : c * 8 + 8], (8, 128)),
                    )
                    * mask2
                    for c in range(2)
                ],
                axis=0,
            )
        )
    spread = jnp.concatenate(split3(jnp.concatenate(spread, axis=1)), axis=0)
    factor = fold3(lax.dot_general(spread, weight2[...], NT, preferred_element_type=F32))
    total = buf2[0]
    for f in range(1, 8):
        total = total + buf2[f]
    update = jnp.concatenate(split3(total * factor), axis=0)
    picked = fold3(lax.dot_general(update, weight3[...], NN, preferred_element_type=F32))
    for s in range(8):
        for h in range(2):
            for c in range(2):
                v = picked[c * 8 : c * 8 + 8, (s * 2 + h) * 128 : (s * 2 + h + 1) * 128] * mask3[h]
                r = s * 4 + c * 2 + h
                src3[r : r + 1, :] = jnp.sum(v, axis=0, keepdims=True)

    own3, whole3 = exchange(2, src3, buf3, lambda s, i: s)
    own3.wait()
    whole3.wait_recv()
    for h in range(2):
        block = jnp.concatenate([buf3[pl.ds(c * 2 + h, 64, stride=4), :] for c in range(2)], axis=0)
        turned[h * 128 : (h + 1) * 128, :] = block.T
    for t in range(TILES):
        lhs = jnp.concatenate(
            [turned[(t * SLOTS + s) * 8 : (t * SLOTS + s + 1) * 8, :] for s in range(SLOTS)], axis=1
        )
        lhs = jnp.concatenate([*split3(lhs), jnp.zeros(lhs.shape, BF16)], axis=0)
        got = lax.dot_general(lhs, halves[t], NN, preferred_element_type=F32)
        got = got[0:8] + got[8:16] + got[16:24]
        got = got[:, 0:128] + got[:, 128:256]
        model_ref[:, t * 128 : (t + 1) * 128] = got[0:PN]
    for p in range(PN):
        upd_ref[p] = turned[pl.ds(6 + 32 * p, 4, stride=8), :]
    whole1.wait_send()
    whole2.wait_send()
    whole3.wait_send()


def local(kernels, basis, support_index, owner_order, precond, damping):
    hbm = pl.BlockSpec(memory_space=pltpu.HBM)
    vmem = pl.BlockSpec(memory_space=pltpu.VMEM)
    points = TILES * 128
    model, update = pl.pallas_call(
        kernel,
        out_shape=(
            jax.ShapeDtypeStruct((PN, points), F32),
            jax.ShapeDtypeStruct((PN, 4, 128), F32),
        ),
        in_specs=[hbm] * 6,
        out_specs=(vmem, vmem),
        scratch_shapes=[
            pltpu.VMEM((PN, 2, points), F32),
            pltpu.VMEM((TILES, SLOTS, 128, 128), F32),
            pltpu.VMEM((1, 128), jnp.int32),
            pltpu.VMEM((PN, 4, 128), F32),
            pltpu.SMEM((SLOTS, TILES), jnp.int32),
            pltpu.SMEM((PN,), F32),
            pltpu.VMEM((TILES, SLOTS * 128, 256), BF16),
            pltpu.VMEM((256, 128), F32),
            pltpu.VMEM((256, 128), F32),
            pltpu.VMEM((256, 128), F32),
            pltpu.VMEM((8, 16, 128), F32),
            pltpu.VMEM((32, 128), F32),
            pltpu.VMEM((256, 128), F32),
            pltpu.VMEM((256, 128), F32),
            pltpu.VMEM((48, 2048), BF16),
            pltpu.VMEM((128, 2048), BF16),
            pltpu.VMEM((128, 2048), BF16),
            pltpu.VMEM((128, 512), BF16),
            pltpu.VMEM((128, 128), F32),
            pltpu.SemaphoreType.DMA((5,)),
            pltpu.SemaphoreType.DMA((TILES,)),
            pltpu.SemaphoreType.DMA((3,)),
            pltpu.SemaphoreType.DMA((3,)),
            pltpu.SemaphoreType.DMA((3,)),
        ],
        compiler_params=pltpu.CompilerParams(
            collective_id=0, has_side_effects=True, vmem_limit_bytes=60 * 1024 * 1024
        ),
        cost_estimate=pl.CostEstimate(flops=10**9, bytes_accessed=2 * 10**6, transcendentals=0),
    )(
        kernels.transpose(1, 0, 2), basis, support_index.T, owner_order.reshape(1, 128),
        precond.transpose(1, 0, 2), damping,
    )
    return model, update.transpose(1, 0, 2)


def solution(mesh):
    in_specs = (
        P("event", None, "mesh"),
        P("mesh", None, None, None),
        P("mesh", None),
        P(),
        P("mesh", None, None),
        P(),
    )
    out_specs = (P(None, "mesh"), P("mesh", None, None))
    return jax.shard_map(local, mesh=mesh, in_specs=in_specs, out_specs=out_specs, check_vma=False)
```

```python
import jax
import jax.numpy as jnp
from jax import lax
from jax.experimental import pallas as pl
from jax.experimental.pallas import tpu as pltpu
from jax.sharding import PartitionSpec as P

MESH = pl.DeviceIdType.MESH
F32 = jnp.float32
BF16 = jnp.bfloat16
TILES = 8
SLOTS = 4
PN = 6
NT = (((1,), (1,)), ((), ()))
NN = (((1,), (0,)), ((), ()))


def split3(v):
    hi = v.astype(BF16)
    rest = v - hi.astype(F32)
    mid = rest.astype(BF16)
    low = (rest - mid.astype(F32)).astype(BF16)
    return hi, mid, low


def iota(shape, dim):
    return lax.broadcasted_iota(jnp.int32, shape, dim)


def fold3(v):
    n = v.shape[0] // 3
    return v[0:n] + v[n : 2 * n] + v[2 * n : 3 * n]


def kernel(
    kern_hbm, basis_hbm, sup_hbm, own_hbm, pre_hbm, damp_hbm,
    model_ref, upd_ref,
    kern_v, basis_v, own_v, pre_v, sup_s, damp_s,
    halves, proj, src1, buf1, buf2, src3, buf3, turned,
    left, weight1, weight3, weight2, key,
    load_sem, tile_sem, send_sem, recv_sem, self_sem,
):
    ev = lax.axis_index("event")
    me = lax.axis_index("mesh")
    x, z0, z1 = lax.rem(ev, 4), lax.rem(lax.div(ev, 4), 2), lax.div(ev, 8)
    core, zh, y = lax.rem(me, 2), lax.rem(lax.div(me, 2), 4), lax.div(me, 8)

    def device(x_, z0_, z1_, core_, zh_, y_):
        return (z1_ * 8 + z0_ * 4 + x_, y_ * 8 + zh_ * 2 + core_)

    xs = [x] + [lax.rem(x + d, 4) for d in (1, 2, 3)]
    ys = [y] + [lax.rem(y + d, 4) for d in (1, 2, 3)]
    cs = [core, 1 - core]
    z0s = [z0, 1 - z0]
    z1s = [z1, 1 - z1]
    zhs = [zh] + [lax.rem(zh + d, 4) for d in (1, 2, 3)]
    slab = y * 2 + core
    mine = slab * 8 + z0 * 4 + x
    far = zh * 2 + z1

    local_peers = []
    for dy in (2, 1, 3, 0):
        for dx in (2, 1, 3, 0):
            for dz in (1, 0):
                for dc in (1, 0):
                    if dy or dx or dz or dc:
                        s = ys[dy] * 2 + cs[dc]
                        i = s * 8 + z0s[dz] * 4 + xs[dx]
                        local_peers.append((device(xs[dx], z0s[dz], z1, cs[dc], zh, ys[dy]), s, i))
    far_peers = [
        device(x, z0, z1s[b], core, zhs[a], y) for a in (2, 1, 3, 0) for b in (1, 0) if a or b
    ]

    barrier = pltpu.get_barrier_semaphore()
    for peer in [p[0] for p in local_peers] + far_peers:
        pl.semaphore_signal(barrier, inc=1, device_id=peer, device_id_type=MESH)

    loads = [
        pltpu.make_async_copy(a, b, load_sem.at[n])
        for n, (a, b) in enumerate(
            ((kern_hbm, kern_v), (pre_hbm, pre_v), (own_hbm, own_v), (sup_hbm, sup_s), (damp_hbm, damp_s))
        )
    ]
    tiles = [pltpu.make_async_copy(basis_hbm.at[t], basis_v.at[t], tile_sem.at[t]) for t in range(TILES)]
    for c in loads:
        c.start()
    for c in tiles:
        c.start()

    row8, lane8 = iota((8, 128), 0), iota((8, 128), 1)
    in8, group = lax.rem(lane8, 8), lax.div(lane8, 8)
    one = lambda c: jnp.where(c, 1.0, 0.0).astype(F32)
    data = (in8 == row8) & (row8 < PN)
    mask1 = [
        one(data | ((in8 == PN) & (row8 == 6))),
        one(data | ((in8 == PN) & (row8 == 7) & (group < 8))),
    ]
    mask3 = [
        one(data | ((in8 == PN) & (lax.div(group, 4) == row8))),
        one(data | ((in8 == PN) & (lax.div(group, 4) + 4 == row8) & (group < 8))),
    ]
    mask2 = one((lax.div(lane8, 32) == lax.rem(row8, 4)) & (row8 < PN))

    nrow, nlane = iota((128, 128), 0), iota((128, 128), 1)
    for a in range(4):
        target = lax.div(lax.rem(nlane, 32), 8) * 32 + a * 8 + lax.rem(nlane, 8)
        weight2[:, a * 128 : (a + 1) * 128] = one(nrow == target).astype(BF16)

    loads[0].wait()
    summed = kern_v[:, 0, :] + kern_v[:, 1, :]
    summed = jnp.concatenate([summed, jnp.zeros((2, summed.shape[1]), F32)], axis=0)
    terms = jnp.concatenate([*split3(summed), jnp.zeros(summed.shape, BF16)], axis=0)

    for t in range(TILES):
        tiles[t].wait()
        part = basis_v[t].reshape(SLOTS * 128, 128)
        hi = part.astype(BF16)
        low = (part - hi.astype(F32)).astype(BF16)
        both = jnp.concatenate([hi, low], axis=1)
        halves[t] = both
        here = terms[:, t * 128 : (t + 1) * 128]
        got = lax.dot_general(jnp.concatenate([here, here], axis=1), both, NT, preferred_element_type=F32)
        got = got[0:8] + got[8:16] + got[16:24]
        for s in range(SLOTS):
            proj[(t * SLOTS + s) * 8 : (t * SLOTS + s + 1) * 8, :] = got[:, s * 128 : (s + 1) * 128]

    for c in loads[1:]:
        c.wait()
    prow = iota((PN, 128), 0)
    damp = jnp.zeros((PN, 128), F32)
    for p in range(PN):
        damp = jnp.where(prow == p, damp_s[p], damp)
    for j in range(4):
        proj[pl.ds(6 + 8 * j, PN, stride=32), :] = -0.125 / (damp + pre_v[:, j, :])
    for t in range(TILES):
        for s in range(SLOTS):
            r = (t * SLOTS + s) * 8 + 7
            proj[r : r + 1, :] = jnp.full((1, 128), sup_s[s, t].astype(F32) * 0.125)

    for h in range(2):
        turn = proj[h * 128 : (h + 1) * 128, :].T
        for c in range(2):
            src1[pl.ds(c * 2 + h, 64, stride=4), :] = turn[c * 64 : (c + 1) * 64]

    owner = jnp.broadcast_to(own_v[...].astype(F32), (128, 128)).T
    key[...] = jnp.where(lax.rem(nlane, 8) == PN, nrow.astype(F32), owner)

    pl.semaphore_wait(barrier, len(local_peers) + len(far_peers))

    def rows(ref, i):
        return ref.at[pl.ds(pl.multiple_of(i * 4, 4), 4), :]

    def exchange(phase, src, dst, pick):
        for dev, s, i in local_peers:
            pltpu.make_async_remote_copy(
                src_ref=rows(src, pick(s, i)),
                dst_ref=rows(dst, mine),
                send_sem=send_sem.at[phase],
                recv_sem=recv_sem.at[phase],
                device_id=dev,
                device_id_type=MESH,
            ).start()
        own = pltpu.make_async_copy(rows(src, pick(slab, mine)), rows(dst, mine), self_sem.at[phase])
        own.start()
        count = 4 * len(local_peers)
        whole = pltpu.make_async_remote_copy(
            src_ref=dst.at[pl.ds(0, count), :],
            dst_ref=dst.at[pl.ds(0, count), :],
            send_sem=send_sem.at[phase],
            recv_sem=recv_sem.at[phase],
            device_id=local_peers[0][0],
            device_id_type=MESH,
        )
        return own, whole

    own1, whole1 = exchange(0, src1, buf1, lambda s, i: i)

    low_lane = iota((1, 128), 1)
    low_in8, low_group = lax.rem(low_lane, 8), lax.div(low_lane, 8)

    own1.wait()
    whole1.wait_recv()
    ids = []
    for s in range(8):
        v = buf1[s * 32 : s * 32 + 8] + buf1[s * 32 + 8 : s * 32 + 16]
        v = v + (buf1[s * 32 + 16 : s * 32 + 24] + buf1[s * 32 + 24 : s * 32 + 32])
        v = v + pltpu.roll(v, 4, 0)
        name = jnp.where(in8 == 7, v, 0.0)
        for d in (1, 2, 4):
            name = name + pltpu.roll(name, 128 - d, 1)
        ids.append(name)
        for h in range(2):
            at = slice((s * 2 + h) * 128, (s * 2 + h + 1) * 128)
            both = jnp.concatenate(
                [jnp.broadcast_to(v[c * 2 + h : c * 2 + h + 1], (8, 128)) * mask1[h] for c in range(2)], axis=0
            )
            left[:, at] = jnp.concatenate(split3(both), axis=0)
            slot = low_group + 16 * h
            code = lax.rem(lax.div(slot, 4), 4) * 32 + s * 4 + lax.rem(slot, 4)
            code = jnp.where(slot < 24, code, -1).astype(F32)
            code = jnp.where(low_in8 == PN, code, name[h : h + 1])
            weight1[:, at] = one(key[...] == code).astype(BF16)
    dense = fold3(lax.dot_general(left[...], weight1[...], NT, preferred_element_type=F32))
    buf2[far] = dense
    for n, dev in enumerate(far_peers):
        pltpu.make_async_remote_copy(
            src_ref=buf2.at[far],
            dst_ref=buf2.at[far],
            send_sem=send_sem.at[1],
            recv_sem=recv_sem.at[1],
            device_id=dev,
            device_id_type=MESH,
        ).start()

    for s in range(8):
        block = (s // 2 * 8 + zh * 2 + s % 2) * 4
        for h in range(2):
            slot = low_group + 16 * h
            code = jnp.where(slot < 24, block + lax.rem(slot, 4), -1).astype(F32)
            code = jnp.where(low_in8 == PN, code, ids[s][h : h + 1])
            weight3[:, (s * 2 + h) * 128 : (s * 2 + h + 1) * 128] = one(key[...] == code).astype(BF16)

    whole2 = pltpu.make_async_remote_copy(
        src_ref=buf2.at[pl.ds(0, 7)],
        dst_ref=buf2.at[pl.ds(0, 7)],
        send_sem=send_sem.at[1],
        recv_sem=recv_sem.at[1],
        device_id=far_peers[0],
        device_id_type=MESH,
    )
    whole2.wait_recv()
    spread = []
    for a in range(4):
        v = buf2[a * 2]
        spread.append(
            jnp.concatenate(
                [
                    jnp.where(
                        row8 < 4,
                        jnp.broadcast_to(v[c * 8 + 6 : c * 8 + 7], (8, 128)),
                        jnp.broadcast_to(v[c * 8 + 7 : c * 8 + 8], (8, 128)),
                    )
                    * mask2
                    for c in range(2)
                ],
                axis=0,
            )
        )
    spread = jnp.concatenate(split3(jnp.concatenate(spread, axis=1)), axis=0)
    factor = fold3(lax.dot_general(spread, weight2[...], NT, preferred_element_type=F32))
    total = buf2[0]
    for f in range(1, 8):
        total = total + buf2[f]
    update = jnp.concatenate(split3(total * factor), axis=0)
    picked = fold3(lax.dot_general(update, weight3[...], NN, preferred_element_type=F32))
    for s in range(8):
        for h in range(2):
            for c in range(2):
                v = picked[c * 8 : c * 8 + 8, (s * 2 + h) * 128 : (s * 2 + h + 1) * 128] * mask3[h]
                r = s * 4 + c * 2 + h
                src3[r : r + 1, :] = jnp.sum(v, axis=0, keepdims=True)

    own3, whole3 = exchange(2, src3, buf3, lambda s, i: s)
    own3.wait()
    whole3.wait_recv()
    for h in range(2):
        block = jnp.concatenate([buf3[pl.ds(c * 2 + h, 64, stride=4), :] for c in range(2)], axis=0)
        turned[h * 128 : (h + 1) * 128, :] = block.T
    for t in range(TILES):
        lhs = jnp.concatenate(
            [turned[(t * SLOTS + s) * 8 : (t * SLOTS + s + 1) * 8, :] for s in range(SLOTS)], axis=1
        )
        lhs = jnp.concatenate([*split3(lhs), jnp.zeros(lhs.shape, BF16)], axis=0)
        got = lax.dot_general(lhs, halves[t], NN, preferred_element_type=F32)
        got = got[0:8] + got[8:16] + got[16:24]
        got = got[:, 0:128] + got[:, 128:256]
        model_ref[:, t * 128 : (t + 1) * 128] = got[0:PN]
    for p in range(PN):
        upd_ref[p] = turned[pl.ds(6 + 32 * p, 4, stride=8), :]
    whole1.wait_send()
    whole2.wait_send()
    whole3.wait_send()


def local(kernels, basis, support_index, owner_order, precond, damping):
    hbm = pl.BlockSpec(memory_space=pltpu.HBM)
    vmem = pl.BlockSpec(memory_space=pltpu.VMEM)
    points = TILES * 128
    model, update = pl.pallas_call(
        kernel,
        out_shape=(
            pltpu.VMEM((PN, points), F32),
            pltpu.VMEM((PN, 4, 128), F32),
        ),
        in_specs=[hbm] * 6,
        out_specs=(vmem, vmem),
        scratch_shapes=[
            pltpu.VMEM((PN, 2, points), F32),
            pltpu.VMEM((TILES, SLOTS, 128, 128), F32),
            pltpu.VMEM((1, 128), jnp.int32),
            pltpu.VMEM((PN, 4, 128), F32),
            pltpu.SMEM((SLOTS, TILES), jnp.int32),
            pltpu.SMEM((PN,), F32),
            pltpu.VMEM((TILES, SLOTS * 128, 256), BF16),
            pltpu.VMEM((256, 128), F32),
            pltpu.VMEM((256, 128), F32),
            pltpu.VMEM((256, 128), F32),
            pltpu.VMEM((8, 16, 128), F32),
            pltpu.VMEM((32, 128), F32),
            pltpu.VMEM((256, 128), F32),
            pltpu.VMEM((256, 128), F32),
            pltpu.VMEM((48, 2048), BF16),
            pltpu.VMEM((128, 2048), BF16),
            pltpu.VMEM((128, 2048), BF16),
            pltpu.VMEM((128, 512), BF16),
            pltpu.VMEM((128, 128), F32),
            pltpu.SemaphoreType.DMA((5,)),
            pltpu.SemaphoreType.DMA((TILES,)),
            pltpu.SemaphoreType.DMA((3,)),
            pltpu.SemaphoreType.DMA((3,)),
            pltpu.SemaphoreType.DMA((3,)),
        ],
        compiler_params=pltpu.CompilerParams(
            collective_id=0, has_side_effects=True, vmem_limit_bytes=60 * 1024 * 1024
        ),
        cost_estimate=pl.CostEstimate(flops=10**9, bytes_accessed=2 * 10**6, transcendentals=0),
    )(
        kernels.transpose(1, 0, 2), basis, support_index.T, owner_order.reshape(1, 128),
        precond.transpose(1, 0, 2), damping,
    )
    return model, update.transpose(1, 0, 2)


def solution(mesh):
    in_specs = (
        P("event", None, "mesh"),
        P("mesh", None, None, None),
        P("mesh", None),
        P(),
        P("mesh", None, None),
        P(),
    )
    out_specs = (P(None, "mesh"), P("mesh", None, None))
    return jax.shard_map(local, mesh=mesh, in_specs=in_specs, out_specs=out_specs, check_vma=False)
```

```python
import jax
import jax.numpy as jnp
from jax import lax
from jax.experimental import pallas as pl
from jax.experimental.pallas import tpu as pltpu
from jax.sharding import PartitionSpec as P

MESH = pl.DeviceIdType.MESH
F32 = jnp.float32
BF16 = jnp.bfloat16
TILES = 8
SLOTS = 4
PN = 6
NT = (((1,), (1,)), ((), ()))
NN = (((1,), (0,)), ((), ()))


def split3(v):
    hi = v.astype(BF16)
    rest = v - hi.astype(F32)
    mid = rest.astype(BF16)
    low = (rest - mid.astype(F32)).astype(BF16)
    return hi, mid, low


def iota(shape, dim):
    return lax.broadcasted_iota(jnp.int32, shape, dim)


def fold3(v):
    n = v.shape[0] // 3
    return v[0:n] + v[n : 2 * n] + v[2 * n : 3 * n]


def kernel(
    kern_hbm, basis_hbm, sup_hbm, own_hbm, pre_hbm, damp_hbm,
    model_ref, upd_ref,
    kern_v, basis_v, own_v, pre_v, sup_s, damp_s,
    halves, proj, src1, buf1, buf2, src3, buf3, turned,
    weight1, weight3, weight4, weight2, key,
    load_sem, tile_sem, send_sem, recv_sem, self_sem,
):
    ev = lax.axis_index("event")
    me = lax.axis_index("mesh")
    x, z0, z1 = lax.rem(ev, 4), lax.rem(lax.div(ev, 4), 2), lax.div(ev, 8)
    core, zh, y = lax.rem(me, 2), lax.rem(lax.div(me, 2), 4), lax.div(me, 8)

    def device(x_, z0_, z1_, core_, zh_, y_):
        return (z1_ * 8 + z0_ * 4 + x_, y_ * 8 + zh_ * 2 + core_)

    xs = [x] + [lax.rem(x + d, 4) for d in (1, 2, 3)]
    ys = [y] + [lax.rem(y + d, 4) for d in (1, 2, 3)]
    cs = [core, 1 - core]
    z0s = [z0, 1 - z0]
    z1s = [z1, 1 - z1]
    zhs = [zh] + [lax.rem(zh + d, 4) for d in (1, 2, 3)]
    slab = y * 2 + core
    mine = slab * 8 + z0 * 4 + x
    far = zh * 2 + z1

    local_peers = []
    for dy in (2, 1, 3, 0):
        for dx in (2, 1, 3, 0):
            for dz in (1, 0):
                for dc in (1, 0):
                    if dy or dx or dz or dc:
                        s = ys[dy] * 2 + cs[dc]
                        i = s * 8 + z0s[dz] * 4 + xs[dx]
                        local_peers.append((device(xs[dx], z0s[dz], z1, cs[dc], zh, ys[dy]), s, i, (2, 1, 3, 0).index(dy) * 2 + 1 - dc, 3 if dx or dz else 4))
    far_peers = [
        device(x, z0, z1s[b], core, zhs[a], y) for a in (2, 1, 3, 0) for b in (1, 0) if a or b
    ]

    loads = [
        pltpu.make_async_copy(a, b, load_sem.at[n])
        for n, (a, b) in enumerate(
            ((kern_hbm, kern_v), (pre_hbm, pre_v), (own_hbm, own_v), (sup_hbm, sup_s), (damp_hbm, damp_s))
        )
    ]
    tiles = [pltpu.make_async_copy(basis_hbm.at[t], basis_v.at[t], tile_sem.at[t]) for t in range(TILES)]
    for c in loads:
        c.start()
    for c in tiles:
        c.start()

    buf1[...] = jnp.zeros(buf1.shape, F32)
    barrier = pltpu.get_barrier_semaphore()
    for peer in [p[0] for p in local_peers] + far_peers:
        pl.semaphore_signal(barrier, inc=1, device_id=peer, device_id_type=MESH)

    row8, lane8 = iota((8, 128), 0), iota((8, 128), 1)
    lane32, quarter = lax.rem(lane8, 32), lax.div(lane8, 32)
    one = lambda c: jnp.where(c, 1.0, 0.0).astype(F32)
    first4 = quarter == row8
    last2 = [(quarter + 4 - 2 * c == row8) & (row8 >= 4) & (row8 < PN) for c in range(2)]
    recips = [
        (quarter == 2 * c) & (lane32 < 24) & (lax.div(lane32, 16) + 6 == row8) for c in range(2)
    ]
    owned = [(quarter == 2 * c) & (lane32 < 24) & (lax.div(lane32, 4) == row8) for c in range(2)]
    mask2 = one((lax.div(lane8, 32) == lax.rem(row8, 4)) & (row8 < PN))

    loads[0].wait()
    summed = kern_v[:, 0, :] + kern_v[:, 1, :]
    summed = jnp.concatenate([summed, jnp.zeros((2, summed.shape[1]), F32)], axis=0)
    terms = jnp.concatenate([*split3(summed), jnp.zeros(summed.shape, BF16)], axis=0)

    for t in range(TILES):
        tiles[t].wait()
        part = basis_v[t].reshape(SLOTS * 128, 128)
        hi = part.astype(BF16)
        low = (part - hi.astype(F32)).astype(BF16)
        both = jnp.concatenate([hi, low], axis=1)
        halves[t] = both
        here = terms[:, t * 128 : (t + 1) * 128]
        got = lax.dot_general(jnp.concatenate([here, here], axis=1), both, NT, preferred_element_type=F32)
        got = got[0:8] + got[8:16] + got[16:24]
        for s in range(SLOTS):
            proj[pl.ds(t * SLOTS + s, PN, stride=32), :] = got[0:PN, s * 128 : (s + 1) * 128]

    for c in loads[1:]:
        c.wait()
    for p in range(PN):
        proj[192 + 4 * p : 196 + 4 * p, :] = -1.0 / (damp_s[p] + pre_v[p])
    proj[216:224, :] = jnp.zeros((8, 128), F32)
    for t in range(TILES):
        for s in range(SLOTS):
            r = 224 + t * SLOTS + s
            proj[r : r + 1, :] = jnp.full((1, 128), sup_s[s, t].astype(F32))

    front = iota((64, 128), 1) < 64
    turn, rest = proj[0:128, :].T, proj[128:256, :].T
    src1[pl.ds(0, 64, stride=4), :] = turn[0:64]
    src1[pl.ds(1, 64, stride=4), :] = turn[64:128]
    src1[pl.ds(2, 64, stride=4), :] = jnp.where(front, rest[0:64], pltpu.roll(rest[64:128], 64, 1))
    src1[pl.ds(3, 64, stride=4), :] = jnp.where(front, pltpu.roll(rest[0:64], 64, 1), rest[64:128])

    pl.semaphore_wait(barrier, len(local_peers) + len(far_peers))

    def rows(ref, i, count=4):
        return ref.at[pl.ds(pl.multiple_of(i * 4, 4), count), :]

    def send(phase, src, dst, dev):
        pltpu.make_async_remote_copy(
            src_ref=src,
            dst_ref=dst,
            send_sem=send_sem.at[phase],
            recv_sem=recv_sem.at[phase],
            device_id=dev,
            device_id_type=MESH,
        ).start()

    def settle(phase, src, dst, count):
        own = pltpu.make_async_copy(src, rows(dst, mine), self_sem.at[phase])
        own.start()
        whole = pltpu.make_async_remote_copy(
            src_ref=dst.at[pl.ds(0, count), :],
            dst_ref=dst.at[pl.ds(0, count), :],
            send_sem=send_sem.at[phase],
            recv_sem=recv_sem.at[phase],
            device_id=local_peers[0][0],
            device_id_type=MESH,
        )
        return own, whole

    total_rows = 0
    for dev, _, i, _, count in local_peers:
        send(0, rows(src1, i, count), rows(buf1, mine, count), dev)
        total_rows += count
    own1, whole1 = settle(0, rows(src1, mine), buf1, total_rows)

    nrow, nlane = iota((128, 128), 0), iota((128, 128), 1)
    for a in range(4):
        target = lax.div(lax.rem(nlane, 32), 8) * 32 + a * 8 + lax.rem(nlane, 8)
        weight2[:, a * 128 : (a + 1) * 128] = one(nrow == target).astype(BF16)
    for s in range(8):
        q = lax.rem(nlane, 32)
        target = lax.rem(lax.div(q, 4), 4) * 32 + s * 4 + lax.rem(q, 4)
        weight4[s] = one((nrow == target) & (q < 24)).astype(BF16)
        target = (s // 2 * 8 + zh * 2 + s % 2) * 4 + lax.rem(q, 4)
        weight3[s] = one((nrow == target) & (q < 24)).astype(BF16)

    owner = jnp.broadcast_to(own_v[...].astype(F32), (128, 128)).T
    key[...] = owner

    own1.wait()
    whole1.wait_recv()
    dense = None
    for s in range(8):
        v = buf1[s * 32 : s * 32 + 8] + buf1[s * 32 + 8 : s * 32 + 16]
        v = v + (buf1[s * 32 + 16 : s * 32 + 24] + buf1[s * 32 + 24 : s * 32 + 32])
        v = v + pltpu.roll(v, 4, 0)
        name = jnp.where(quarter == 1, v, 0.0)
        name = name + pltpu.roll(name, 32, 1)
        name = name + pltpu.roll(name, 64, 1)
        pick = one(key[...] == name[3:4]).astype(BF16)
        weight1[s] = pick
        row = [jnp.broadcast_to(v[k : k + 1], (8, 128)) for k in range(4)]
        both = [
            [jnp.where(first4, row[c], jnp.where(last2[c], row[2], 0.0)) for c in range(2)],
            [jnp.where(recips[c], row[3], 0.0) for c in range(2)],
        ]
        left = jnp.concatenate([jnp.concatenate(b, axis=0) for b in both], axis=1)
        got = lax.dot_general(
            jnp.concatenate(split3(left), axis=0),
            jnp.concatenate([pick, weight4[s]], axis=1),
            NT,
            preferred_element_type=F32,
        )
        dense = got if dense is None else dense + got
    buf2[far] = fold3(dense)
    for n, dev in enumerate(far_peers):
        pltpu.make_async_remote_copy(
            src_ref=buf2.at[far],
            dst_ref=buf2.at[far],
            send_sem=send_sem.at[1],
            recv_sem=recv_sem.at[1],
            device_id=dev,
            device_id_type=MESH,
        ).start()

    whole2 = pltpu.make_async_remote_copy(
        src_ref=buf2.at[pl.ds(0, 7)],
        dst_ref=buf2.at[pl.ds(0, 7)],
        send_sem=send_sem.at[1],
        recv_sem=recv_sem.at[1],
        device_id=far_peers[0],
        device_id_type=MESH,
    )
    whole2.wait_recv()
    spread = []
    for a in range(4):
        v = buf2[a * 2]
        spread.append(
            jnp.concatenate(
                [
                    jnp.where(
                        row8 < 4,
                        jnp.broadcast_to(v[c * 8 + 6 : c * 8 + 7], (8, 128)),
                        jnp.broadcast_to(v[c * 8 + 7 : c * 8 + 8], (8, 128)),
                    )
                    * mask2
                    for c in range(2)
                ],
                axis=0,
            )
        )
    spread = jnp.concatenate(split3(jnp.concatenate(spread, axis=1)), axis=0)
    factor = fold3(lax.dot_general(spread, weight2[...], NT, preferred_element_type=F32))
    total = buf2[0]
    for f in range(1, 8):
        total = total + buf2[f]
    update = jnp.concatenate(split3(total * factor), axis=0)
    for g in range(8):
        s = ys[(2, 1, 3, 0)[g // 2]] * 2 + cs[1 - g % 2]
        pair = jnp.concatenate([weight1[s], weight3[s]], axis=1)
        picked = fold3(lax.dot_general(update, pair, NN, preferred_element_type=F32))
        a = [picked[c * 8 : c * 8 + 8, 0:128] for c in range(2)]
        o = [jnp.where(owned[c], picked[c * 8 : c * 8 + 8, 128:256], 0.0) for c in range(2)]
        out = [jnp.where(first4, a[0], 0.0), jnp.where(first4, a[1], 0.0)]
        out.append(jnp.where(last2[0], a[0], 0.0) + jnp.where(last2[1], a[1], 0.0))
        out.append(o[0] + o[1])
        for k in range(4):
            src3[g * 4 + k : g * 4 + k + 1, :] = jnp.sum(out[k], axis=0, keepdims=True)
    for dev, _, _, g, _ in local_peers:
        send(2, src3.at[pl.ds(g * 4, 4), :], rows(buf3, mine), dev)
    own3, whole3 = settle(2, src3.at[pl.ds(28, 4), :], buf3, 4 * len(local_peers))
    own3.wait()
    whole3.wait_recv()
    part = [buf3[pl.ds(k, 64, stride=4), :] for k in range(4)]
    turned[0:128, :] = jnp.concatenate(part[0:2], axis=0).T
    rest = [
        jnp.where(front, part[2], pltpu.roll(part[3], 64, 1)),
        jnp.where(front, pltpu.roll(part[2], 64, 1), part[3]),
    ]
    turned[128:256, :] = jnp.concatenate(rest, axis=0).T
    for t in range(TILES):
        lhs = jnp.concatenate([turned[pl.ds(t * SLOTS + s, 8, stride=32), :] for s in range(SLOTS)], axis=1)
        lhs = jnp.concatenate([*split3(lhs), jnp.zeros(lhs.shape, BF16)], axis=0)
        got = lax.dot_general(lhs, halves[t], NN, preferred_element_type=F32)
        got = got[0:8] + got[8:16] + got[16:24]
        got = got[:, 0:128] + got[:, 128:256]
        model_ref[:, t * 128 : (t + 1) * 128] = got[0:PN]
    for p in range(PN):
        upd_ref[p] = turned[192 + 4 * p : 196 + 4 * p, :]
    whole1.wait_send()
    whole2.wait_send()
    whole3.wait_send()


def local(kernels, basis, support_index, owner_order, precond, damping):
    hbm = pl.BlockSpec(memory_space=pltpu.HBM)
    vmem = pl.BlockSpec(memory_space=pltpu.VMEM)
    points = TILES * 128
    model, update = pl.pallas_call(
        kernel,
        out_shape=(
            pltpu.VMEM((PN, points), F32),
            pltpu.VMEM((PN, 4, 128), F32),
        ),
        in_specs=[hbm] * 6,
        out_specs=(vmem, vmem),
        scratch_shapes=[
            pltpu.VMEM((PN, 2, points), F32),
            pltpu.VMEM((TILES, SLOTS, 128, 128), F32),
            pltpu.VMEM((1, 128), jnp.int32),
            pltpu.VMEM((PN, 4, 128), F32),
            pltpu.SMEM((SLOTS, TILES), jnp.int32),
            pltpu.SMEM((PN,), F32),
            pltpu.VMEM((TILES, SLOTS * 128, 256), BF16),
            pltpu.VMEM((256, 128), F32),
            pltpu.VMEM((256, 128), F32),
            pltpu.VMEM((256, 128), F32),
            pltpu.VMEM((8, 16, 128), F32),
            pltpu.VMEM((32, 128), F32),
            pltpu.VMEM((256, 128), F32),
            pltpu.VMEM((256, 128), F32),
            pltpu.VMEM((8, 128, 128), BF16),
            pltpu.VMEM((8, 128, 128), BF16),
            pltpu.VMEM((8, 128, 128), BF16),
            pltpu.VMEM((128, 512), BF16),
            pltpu.VMEM((128, 128), F32),
            pltpu.SemaphoreType.DMA((5,)),
            pltpu.SemaphoreType.DMA((TILES,)),
            pltpu.SemaphoreType.DMA((3,)),
            pltpu.SemaphoreType.DMA((3,)),
            pltpu.SemaphoreType.DMA((3,)),
        ],
        compiler_params=pltpu.CompilerParams(
            collective_id=0, has_side_effects=True, vmem_limit_bytes=60 * 1024 * 1024
        ),
        cost_estimate=pl.CostEstimate(flops=10**9, bytes_accessed=2 * 10**6, transcendentals=0),
    )(
        kernels.transpose(1, 0, 2), basis, support_index.T, owner_order.reshape(1, 128),
        precond.transpose(1, 0, 2), damping,
    )
    return model, update.transpose(1, 0, 2)


def solution(mesh):
    in_specs = (
        P("event", None, "mesh"),
        P("mesh", None, None, None),
        P("mesh", None),
        P(),
        P("mesh", None, None),
        P(),
    )
    out_specs = (P(None, "mesh"), P("mesh", None, None))
    return jax.shard_map(local, mesh=mesh, in_specs=in_specs, out_specs=out_specs, check_vma=False)
```

```python
import jax
import jax.numpy as jnp
from jax import lax
from jax.experimental import pallas as pl
from jax.experimental.pallas import tpu as pltpu
from jax.sharding import PartitionSpec as P

MESH = pl.DeviceIdType.MESH
F32 = jnp.float32
BF16 = jnp.bfloat16
TILES = 8
SLOTS = 4
PN = 6
NT = (((1,), (1,)), ((), ()))
NN = (((1,), (0,)), ((), ()))


def split3(v):
    hi = v.astype(BF16)
    rest = v - hi.astype(F32)
    mid = rest.astype(BF16)
    low = (rest - mid.astype(F32)).astype(BF16)
    return hi, mid, low


def iota(shape, dim):
    return lax.broadcasted_iota(jnp.int32, shape, dim)


def fold3(v):
    n = v.shape[0] // 3
    return v[0:n] + v[n : 2 * n] + v[2 * n : 3 * n]


def kernel(
    kern_hbm, basis_hbm, sup_hbm, own_hbm, pre_hbm, damp_hbm,
    model_ref, upd_ref,
    kern_v, basis_v, own_v, pre_v, sup_s, damp_s,
    halves, proj, src1, buf1, buf2, src3, buf3, turned,
    weight1, weight3, weight4, weight2, key,
    load_sem, tile_sem, send_sem, recv_sem, self_sem,
):
    ev = lax.axis_index("event")
    me = lax.axis_index("mesh")
    x, z0, z1 = lax.rem(ev, 4), lax.rem(lax.div(ev, 4), 2), lax.div(ev, 8)
    core, zh, y = lax.rem(me, 2), lax.rem(lax.div(me, 2), 4), lax.div(me, 8)

    def device(x_, z0_, z1_, core_, zh_, y_):
        return (z1_ * 8 + z0_ * 4 + x_, y_ * 8 + zh_ * 2 + core_)

    xs = [x] + [lax.rem(x + d, 4) for d in (1, 2, 3)]
    ys = [y] + [lax.rem(y + d, 4) for d in (1, 2, 3)]
    cs = [core, 1 - core]
    z0s = [z0, 1 - z0]
    z1s = [z1, 1 - z1]
    zhs = [zh] + [lax.rem(zh + d, 4) for d in (1, 2, 3)]
    slab = y * 2 + core
    mine = slab * 8 + z0 * 4 + x
    far = zh * 2 + z1

    local_peers = []
    for dy in (2, 1, 3, 0):
        for dx in (2, 1, 3, 0):
            for dz in (1, 0):
                for dc in (1, 0):
                    if dy or dx or dz or dc:
                        s = ys[dy] * 2 + cs[dc]
                        i = s * 8 + z0s[dz] * 4 + xs[dx]
                        local_peers.append((device(xs[dx], z0s[dz], z1, cs[dc], zh, ys[dy]), s, i, (2, 1, 3, 0).index(dy) * 2 + 1 - dc, 3 if dx or dz else 4))
    far_peers = [
        device(x, z0, z1s[b], core, zhs[a], y) for a in (2, 1, 3, 0) for b in (1, 0) if a or b
    ]

    loads = [
        pltpu.make_async_copy(a, b, load_sem.at[n])
        for n, (a, b) in enumerate(
            ((kern_hbm, kern_v), (pre_hbm, pre_v), (own_hbm, own_v), (sup_hbm, sup_s), (damp_hbm, damp_s))
        )
    ]
    tiles = [pltpu.make_async_copy(basis_hbm.at[t], basis_v.at[t], tile_sem.at[t]) for t in range(TILES)]
    for c in loads:
        c.start()
    for c in tiles:
        c.start()

    buf1[...] = jnp.zeros(buf1.shape, F32)
    barrier = pltpu.get_barrier_semaphore()
    for peer in [p[0] for p in local_peers] + far_peers:
        pl.semaphore_signal(barrier, inc=1, device_id=peer, device_id_type=MESH)

    row8, lane8 = iota((8, 128), 0), iota((8, 128), 1)
    lane32, quarter = lax.rem(lane8, 32), lax.div(lane8, 32)
    one = lambda c: jnp.where(c, 1.0, 0.0).astype(F32)
    first4 = quarter == row8
    last2 = [(quarter + 4 - 2 * c == row8) & (row8 >= 4) & (row8 < PN) for c in range(2)]
    recips = [
        (quarter == 2 * c) & (lane32 < 24) & (lax.div(lane32, 16) + 6 == row8) for c in range(2)
    ]
    owned = [(quarter == 2 * c) & (lane32 < 24) & (lax.div(lane32, 4) == row8) for c in range(2)]
    mask2 = one((lax.div(lane8, 32) == lax.rem(row8, 4)) & (row8 < PN))

    loads[0].wait()
    summed = kern_v[:, 0, :] + kern_v[:, 1, :]
    summed = jnp.concatenate([summed, jnp.zeros((2, summed.shape[1]), F32)], axis=0)
    terms = jnp.concatenate([*split3(summed), jnp.zeros(summed.shape, BF16)], axis=0)

    for t in range(TILES):
        tiles[t].wait()
        part = basis_v[t].reshape(SLOTS * 128, 128)
        hi = part.astype(BF16)
        low = (part - hi.astype(F32)).astype(BF16)
        both = jnp.concatenate([hi, low], axis=1)
        halves[t] = both
        here = terms[:, t * 128 : (t + 1) * 128]
        got = lax.dot_general(jnp.concatenate([here, here], axis=1), both, NT, preferred_element_type=F32)
        got = got[0:8] + got[8:16] + got[16:24]
        for s in range(SLOTS):
            proj[pl.ds(t * SLOTS + s, PN, stride=32), :] = got[0:PN, s * 128 : (s + 1) * 128]

    for c in loads[1:]:
        c.wait()
    for p in range(PN):
        proj[192 + 4 * p : 196 + 4 * p, :] = -1.0 / (damp_s[p] + pre_v[p])
    proj[216:224, :] = jnp.zeros((8, 128), F32)
    for t in range(TILES):
        for s in range(SLOTS):
            r = 224 + t * SLOTS + s
            proj[r : r + 1, :] = jnp.full((1, 128), sup_s[s, t].astype(F32))

    front = iota((64, 128), 1) < 64
    turn, rest = proj[0:128, :].T, proj[128:256, :].T
    src1[pl.ds(0, 64, stride=4), :] = turn[0:64]
    src1[pl.ds(1, 64, stride=4), :] = turn[64:128]
    src1[pl.ds(2, 64, stride=4), :] = jnp.where(front, rest[0:64], pltpu.roll(rest[64:128], 64, 1))
    src1[pl.ds(3, 64, stride=4), :] = jnp.where(front, pltpu.roll(rest[0:64], 64, 1), rest[64:128])

    pl.semaphore_wait(barrier, len(local_peers) + len(far_peers))

    def rows(ref, i, count=4):
        return ref.at[pl.ds(pl.multiple_of(i * 4, 4), count), :]

    def send(phase, src, dst, dev):
        pltpu.make_async_remote_copy(
            src_ref=src,
            dst_ref=dst,
            send_sem=send_sem.at[phase],
            recv_sem=recv_sem.at[phase],
            device_id=dev,
            device_id_type=MESH,
        ).start()

    def settle(phase, src, dst, count):
        own = pltpu.make_async_copy(src, rows(dst, mine), self_sem.at[phase])
        own.start()
        whole = pltpu.make_async_remote_copy(
            src_ref=dst.at[pl.ds(0, count), :],
            dst_ref=dst.at[pl.ds(0, count), :],
            send_sem=send_sem.at[phase],
            recv_sem=recv_sem.at[phase],
            device_id=local_peers[0][0],
            device_id_type=MESH,
        )
        return own, whole

    total_rows = 0
    for dev, _, i, _, count in local_peers:
        send(0, rows(src1, i, count), rows(buf1, mine, count), dev)
        total_rows += count
    own1, whole1 = settle(0, rows(src1, mine), buf1, total_rows)

    nrow, nlane = iota((128, 128), 0), iota((128, 128), 1)
    for a in range(4):
        target = lax.div(lax.rem(nlane, 32), 8) * 32 + a * 8 + lax.rem(nlane, 8)
        weight2[:, a * 128 : (a + 1) * 128] = one(nrow == target).astype(BF16)
    for s in range(8):
        q = lax.rem(nlane, 32)
        target = lax.rem(lax.div(q, 4), 4) * 32 + s * 4 + lax.rem(q, 4)
        weight4[s] = one((nrow == target) & (q < 24)).astype(BF16)
        target = (s // 2 * 8 + zh * 2 + s % 2) * 4 + lax.rem(q, 4)
        weight3[s] = one((nrow == target) & (q < 24)).astype(BF16)

    owner = jnp.broadcast_to(own_v[...].astype(F32), (128, 128)).T
    key[...] = owner

    own1.wait()
    whole1.wait_recv()
    dense = None
    for s in range(8):
        v = buf1[s * 32 : s * 32 + 8] + buf1[s * 32 + 8 : s * 32 + 16]
        v = v + (buf1[s * 32 + 16 : s * 32 + 24] + buf1[s * 32 + 24 : s * 32 + 32])
        v = v + pltpu.roll(v, 4, 0)
        name = jnp.where(quarter == 1, v, 0.0)
        name = name + pltpu.roll(name, 32, 1)
        name = name + pltpu.roll(name, 64, 1)
        pick = one(key[...] == name[3:4]).astype(BF16)
        weight1[s] = pick
        row = [jnp.broadcast_to(v[k : k + 1], (8, 128)) for k in range(4)]
        both = [
            [jnp.where(first4, row[c], jnp.where(last2[c], row[2], 0.0)) for c in range(2)],
            [jnp.where(recips[c], row[3], 0.0) for c in range(2)],
        ]
        left = jnp.concatenate([jnp.concatenate(b, axis=0) for b in both], axis=1)
        got = lax.dot_general(
            jnp.concatenate(split3(left), axis=0),
            jnp.concatenate([pick, weight4[s]], axis=1),
            NT,
            preferred_element_type=F32,
        )
        dense = got if dense is None else dense + got
    buf2[far] = fold3(dense)
    for n, dev in enumerate(far_peers):
        pltpu.make_async_remote_copy(
            src_ref=buf2.at[far],
            dst_ref=buf2.at[far],
            send_sem=send_sem.at[1],
            recv_sem=recv_sem.at[1],
            device_id=dev,
            device_id_type=MESH,
        ).start()

    whole2 = pltpu.make_async_remote_copy(
        src_ref=buf2.at[pl.ds(0, 7)],
        dst_ref=buf2.at[pl.ds(0, 7)],
        send_sem=send_sem.at[1],
        recv_sem=recv_sem.at[1],
        device_id=far_peers[0],
        device_id_type=MESH,
    )
    whole2.wait_recv()
    spread = []
    for a in range(4):
        v = buf2[a * 2]
        spread.append(
            jnp.concatenate(
                [
                    jnp.where(
                        row8 < 4,
                        jnp.broadcast_to(v[c * 8 + 6 : c * 8 + 7], (8, 128)),
                        jnp.broadcast_to(v[c * 8 + 7 : c * 8 + 8], (8, 128)),
                    )
                    * mask2
                    for c in range(2)
                ],
                axis=0,
            )
        )
    spread = jnp.concatenate(split3(jnp.concatenate(spread, axis=1)), axis=0)
    factor = fold3(lax.dot_general(spread, weight2[...], NT, preferred_element_type=F32))
    total = buf2[0]
    for f in range(1, 8):
        total = total + buf2[f]
    update = jnp.concatenate(split3(total * factor), axis=0)
    for g in range(8):
        s = ys[(2, 1, 3, 0)[g // 2]] * 2 + cs[1 - g % 2]
        pair = jnp.concatenate([weight1[s], weight3[s]], axis=1)
        picked = fold3(lax.dot_general(update, pair, NN, preferred_element_type=F32))
        a = [picked[c * 8 : c * 8 + 8, 0:128] for c in range(2)]
        o = [jnp.where(owned[c], picked[c * 8 : c * 8 + 8, 128:256], 0.0) for c in range(2)]
        out = [jnp.where(first4, a[0], 0.0), jnp.where(first4, a[1], 0.0)]
        out.append(jnp.where(last2[0], a[0], 0.0) + jnp.where(last2[1], a[1], 0.0))
        out.append(o[0] + o[1])
        for k in range(4):
            src3[g * 4 + k : g * 4 + k + 1, :] = jnp.sum(out[k], axis=0, keepdims=True)
    for dev, _, _, g, _ in local_peers:
        send(2, src3.at[pl.ds(g * 4, 4), :], rows(buf3, mine), dev)
    own3, whole3 = settle(2, src3.at[pl.ds(28, 4), :], buf3, 4 * len(local_peers))
    own3.wait()
    whole3.wait_recv()
    part = [buf3[pl.ds(k, 64, stride=4), :] for k in range(4)]
    turned[0:128, :] = jnp.concatenate(part[0:2], axis=0).T
    rest = [
        jnp.where(front, part[2], pltpu.roll(part[3], 64, 1)),
        jnp.where(front, pltpu.roll(part[2], 64, 1), part[3]),
    ]
    turned[128:256, :] = jnp.concatenate(rest, axis=0).T
    for t in range(TILES):
        lhs = jnp.concatenate([turned[pl.ds(t * SLOTS + s, 8, stride=32), :] for s in range(SLOTS)], axis=1)
        lhs = jnp.concatenate([*split3(lhs), jnp.zeros(lhs.shape, BF16)], axis=0)
        got = lax.dot_general(lhs, halves[t], NN, preferred_element_type=F32)
        got = got[0:8] + got[8:16] + got[16:24]
        got = got[:, 0:128] + got[:, 128:256]
        model_ref[:, t * 128 : (t + 1) * 128] = got[0:PN]
    for p in range(PN):
        upd_ref[p] = turned[192 + 4 * p : 196 + 4 * p, :]
    whole1.wait_send()
    whole2.wait_send()
    whole3.wait_send()


def local(kernels, basis, support_index, owner_order, precond, damping):
    hbm = pl.BlockSpec(memory_space=pltpu.HBM)
    vmem = pl.BlockSpec(memory_space=pltpu.VMEM)
    points = TILES * 128
    model, update = pl.pallas_call(
        kernel,
        out_shape=(
            pltpu.VMEM((PN, points), F32),
            pltpu.VMEM((PN, 4, 128), F32),
        ),
        in_specs=[hbm] * 6,
        out_specs=(vmem, vmem),
        scratch_shapes=[
            pltpu.VMEM((PN, 2, points), F32),
            pltpu.VMEM((TILES, SLOTS, 128, 128), F32),
            pltpu.VMEM((1, 128), jnp.int32),
            pltpu.VMEM((PN, 4, 128), F32),
            pltpu.SMEM((SLOTS, TILES), jnp.int32),
            pltpu.SMEM((PN,), F32),
            pltpu.VMEM((TILES, SLOTS * 128, 256), BF16),
            pltpu.VMEM((288, 128), F32),
            pltpu.VMEM((264, 128), F32),
            pltpu.VMEM((256, 128), F32),
            pltpu.VMEM((8, 16, 128), F32),
            pltpu.VMEM((32, 128), F32),
            pltpu.VMEM((264, 128), F32),
            pltpu.VMEM((288, 128), F32),
            pltpu.VMEM((8, 128, 128), BF16),
            pltpu.VMEM((8, 128, 128), BF16),
            pltpu.VMEM((8, 128, 128), BF16),
            pltpu.VMEM((128, 512), BF16),
            pltpu.VMEM((128, 128), F32),
            pltpu.SemaphoreType.DMA((5,)),
            pltpu.SemaphoreType.DMA((TILES,)),
            pltpu.SemaphoreType.DMA((3,)),
            pltpu.SemaphoreType.DMA((3,)),
            pltpu.SemaphoreType.DMA((3,)),
        ],
        compiler_params=pltpu.CompilerParams(
            collective_id=0, has_side_effects=True, vmem_limit_bytes=60 * 1024 * 1024
        ),
        cost_estimate=pl.CostEstimate(flops=10**9, bytes_accessed=2 * 10**6, transcendentals=0),
    )(
        kernels.transpose(1, 0, 2), basis, support_index.T, owner_order.reshape(1, 128),
        precond.transpose(1, 0, 2), damping,
    )
    return model, update.transpose(1, 0, 2)


def solution(mesh):
    in_specs = (
        P("event", None, "mesh"),
        P("mesh", None, None, None),
        P("mesh", None),
        P(),
        P("mesh", None, None),
        P(),
    )
    out_specs = (P(None, "mesh"), P("mesh", None, None))
    return jax.shard_map(local, mesh=mesh, in_specs=in_specs, out_specs=out_specs, check_vma=False)
```

```python
import jax
import jax.numpy as jnp
from jax import lax
from jax.experimental import pallas as pl
from jax.experimental.pallas import tpu as pltpu
from jax.sharding import PartitionSpec as P

MESH = pl.DeviceIdType.MESH
F32 = jnp.float32
BF16 = jnp.bfloat16
TILES = 8
SLOTS = 4
PN = 6
NT = (((1,), (1,)), ((), ()))
NN = (((1,), (0,)), ((), ()))


def split3(v):
    hi = v.astype(BF16)
    rest = v - hi.astype(F32)
    mid = rest.astype(BF16)
    low = (rest - mid.astype(F32)).astype(BF16)
    return hi, mid, low


def iota(shape, dim):
    return lax.broadcasted_iota(jnp.int32, shape, dim)


def fold3(v):
    n = v.shape[0] // 3
    return v[0:n] + v[n : 2 * n] + v[2 * n : 3 * n]


def kernel(
    kern_hbm, basis_hbm, sup_hbm, own_hbm, pre_hbm, damp_hbm,
    model_ref, upd_ref,
    kern_v, basis_v, own_v, pre_v, sup_s, damp_s,
    halves, proj, src1, buf1, buf2, src3, buf3, turned,
    weight1, weight3, weight4, weight2, key,
    load_sem, tile_sem, send_sem, recv_sem, self_sem,
):
    ev = lax.axis_index("event")
    me = lax.axis_index("mesh")
    x, z0, z1 = lax.rem(ev, 4), lax.rem(lax.div(ev, 4), 2), lax.div(ev, 8)
    core, zh, y = lax.rem(me, 2), lax.rem(lax.div(me, 2), 4), lax.div(me, 8)

    def device(x_, z0_, z1_, core_, zh_, y_):
        return (z1_ * 8 + z0_ * 4 + x_, y_ * 8 + zh_ * 2 + core_)

    xs = [x] + [lax.rem(x + d, 4) for d in (1, 2, 3)]
    ys = [y] + [lax.rem(y + d, 4) for d in (1, 2, 3)]
    cs = [core, 1 - core]
    z0s = [z0, 1 - z0]
    z1s = [z1, 1 - z1]
    zhs = [zh] + [lax.rem(zh + d, 4) for d in (1, 2, 3)]
    slab = y * 2 + core
    mine = slab * 8 + z0 * 4 + x
    far = zh * 2 + z1

    local_peers = []
    for dy in (2, 1, 3, 0):
        for dx in (2, 1, 3, 0):
            for dz in (1, 0):
                for dc in (1, 0):
                    if dy or dx or dz or dc:
                        s = ys[dy] * 2 + cs[dc]
                        i = s * 8 + z0s[dz] * 4 + xs[dx]
                        local_peers.append((device(xs[dx], z0s[dz], z1, cs[dc], zh, ys[dy]), s, i, (2, 1, 3, 0).index(dy) * 2 + 1 - dc, 3 if dx or dz else 4))
    far_peers = [
        device(x, z0, z1s[b], core, zhs[a], y) for a in (2, 1, 3, 0) for b in (1, 0) if a or b
    ]

    loads = [
        pltpu.make_async_copy(a, b, load_sem.at[n])
        for n, (a, b) in enumerate(
            ((kern_hbm, kern_v), (pre_hbm, pre_v), (own_hbm, own_v), (sup_hbm, sup_s), (damp_hbm, damp_s))
        )
    ]
    tiles = [pltpu.make_async_copy(basis_hbm.at[t], basis_v.at[t], tile_sem.at[t]) for t in range(TILES)]
    for c in loads:
        c.start()
    for c in tiles:
        c.start()

    buf1[...] = jnp.zeros(buf1.shape, F32)
    barrier = pltpu.get_barrier_semaphore()
    for peer in [p[0] for p in local_peers] + far_peers:
        pl.semaphore_signal(barrier, inc=1, device_id=peer, device_id_type=MESH)

    row8, lane8 = iota((8, 128), 0), iota((8, 128), 1)
    lane32, quarter = lax.rem(lane8, 32), lax.div(lane8, 32)
    one = lambda c: jnp.where(c, 1.0, 0.0).astype(F32)
    first4 = quarter == row8
    last2 = [(quarter + 4 - 2 * c == row8) & (row8 >= 4) & (row8 < PN) for c in range(2)]
    recips = [
        (quarter == 2 * c) & (lane32 < 24) & (lax.div(lane32, 16) + 6 == row8) for c in range(2)
    ]
    owned = [(quarter == 2 * c) & (lane32 < 24) & (lax.div(lane32, 4) == row8) for c in range(2)]
    mask2 = one((lax.div(lane8, 32) == lax.rem(row8, 4)) & (row8 < PN))

    loads[0].wait()
    summed = kern_v[:, 0, :] + kern_v[:, 1, :]
    summed = jnp.concatenate([summed, jnp.zeros((2, summed.shape[1]), F32)], axis=0)
    terms = jnp.concatenate([*split3(summed), jnp.zeros(summed.shape, BF16)], axis=0)

    for t in range(TILES):
        tiles[t].wait()
        part = basis_v[t].reshape(SLOTS * 128, 128)
        hi = part.astype(BF16)
        low = (part - hi.astype(F32)).astype(BF16)
        both = jnp.concatenate([hi, low], axis=1)
        halves[t] = both
        here = terms[:, t * 128 : (t + 1) * 128]
        got = lax.dot_general(jnp.concatenate([here, here], axis=1), both, NT, preferred_element_type=F32)
        got = got[0:8] + got[8:16] + got[16:24]
        for s in range(SLOTS):
            proj[pl.ds(t * SLOTS + s, PN, stride=32), :] = got[0:PN, s * 128 : (s + 1) * 128]

    for c in loads[1:]:
        c.wait()
    for p in range(PN):
        proj[192 + 4 * p : 196 + 4 * p, :] = -1.0 / (damp_s[p] + pre_v[p])
    proj[216:224, :] = jnp.zeros((8, 128), F32)
    for t in range(TILES):
        for s in range(SLOTS):
            r = 224 + t * SLOTS + s
            proj[r : r + 1, :] = jnp.full((1, 128), sup_s[s, t].astype(F32))

    front = iota((64, 128), 1) < 64
    turn, rest = proj[0:128, :].T, proj[128:256, :].T
    src1[pl.ds(0, 64, stride=4), :] = turn[0:64]
    src1[pl.ds(1, 64, stride=4), :] = turn[64:128]
    src1[pl.ds(2, 64, stride=4), :] = jnp.where(front, rest[0:64], pltpu.roll(rest[64:128], 64, 1))
    src1[pl.ds(3, 64, stride=4), :] = jnp.where(front, pltpu.roll(rest[0:64], 64, 1), rest[64:128])

    pl.semaphore_wait(barrier, len(local_peers) + len(far_peers))

    def rows(ref, i, count=4):
        return ref.at[pl.ds(pl.multiple_of(i * 4, 4), count), :]

    def send(phase, src, dst, dev):
        pltpu.make_async_remote_copy(
            src_ref=src,
            dst_ref=dst,
            send_sem=send_sem.at[phase],
            recv_sem=recv_sem.at[phase],
            device_id=dev,
            device_id_type=MESH,
        ).start()

    def settle(phase, src, dst, count):
        own = pltpu.make_async_copy(src, rows(dst, mine), self_sem.at[phase])
        own.start()
        whole = pltpu.make_async_remote_copy(
            src_ref=dst.at[pl.ds(0, count), :],
            dst_ref=dst.at[pl.ds(0, count), :],
            send_sem=send_sem.at[phase],
            recv_sem=recv_sem.at[phase],
            device_id=local_peers[0][0],
            device_id_type=MESH,
        )
        return own, whole

    total_rows = 0
    for dev, _, i, _, count in local_peers:
        send(0, rows(src1, i, count), rows(buf1, mine, count), dev)
        total_rows += count
    own1, whole1 = settle(0, rows(src1, mine), buf1, total_rows)

    nrow, nlane = iota((128, 128), 0), iota((128, 128), 1)
    for a in range(4):
        target = lax.div(lax.rem(nlane, 32), 8) * 32 + a * 8 + lax.rem(nlane, 8)
        weight2[:, a * 128 : (a + 1) * 128] = one(nrow == target).astype(BF16)
    for s in range(8):
        q = lax.rem(nlane, 32)
        target = lax.rem(lax.div(q, 4), 4) * 32 + s * 4 + lax.rem(q, 4)
        weight4[s] = one((nrow == target) & (q < 24)).astype(BF16)
        target = (s // 2 * 8 + zh * 2 + s % 2) * 4 + lax.rem(q, 4)
        weight3[s] = one((nrow == target) & (q < 24)).astype(BF16)

    owner = jnp.broadcast_to(own_v[...].astype(F32), (128, 128)).T
    key[...] = owner

    own1.wait()
    whole1.wait_recv()
    dense = None
    for s in range(8):
        v = buf1[s * 32 : s * 32 + 8] + buf1[s * 32 + 8 : s * 32 + 16]
        v = v + (buf1[s * 32 + 16 : s * 32 + 24] + buf1[s * 32 + 24 : s * 32 + 32])
        v = v + pltpu.roll(v, 4, 0)
        name = jnp.where(quarter == 1, v, 0.0)
        name = name + pltpu.roll(name, 32, 1)
        name = name + pltpu.roll(name, 64, 1)
        pick = one(key[...] == name[3:4]).astype(BF16)
        weight1[s] = pick
        row = [jnp.broadcast_to(v[k : k + 1], (8, 128)) for k in range(4)]
        both = [
            [jnp.where(first4, row[c], jnp.where(last2[c], row[2], 0.0)) for c in range(2)],
            [jnp.where(recips[c], row[3], 0.0) for c in range(2)],
        ]
        left = jnp.concatenate([jnp.concatenate(b, axis=0) for b in both], axis=1)
        got = lax.dot_general(
            jnp.concatenate(split3(left), axis=0),
            jnp.concatenate([pick, weight4[s]], axis=1),
            NT,
            preferred_element_type=F32,
        )
        dense = got if dense is None else dense + got
    buf2[far] = fold3(dense)
    for n, dev in enumerate(far_peers):
        pltpu.make_async_remote_copy(
            src_ref=buf2.at[far],
            dst_ref=buf2.at[far],
            send_sem=send_sem.at[1],
            recv_sem=recv_sem.at[1],
            device_id=dev,
            device_id_type=MESH,
        ).start()

    whole2 = pltpu.make_async_remote_copy(
        src_ref=buf2.at[pl.ds(0, 7)],
        dst_ref=buf2.at[pl.ds(0, 7)],
        send_sem=send_sem.at[1],
        recv_sem=recv_sem.at[1],
        device_id=far_peers[0],
        device_id_type=MESH,
    )
    whole2.wait_recv()
    spread = []
    for a in range(4):
        v = buf2[a * 2]
        spread.append(
            jnp.concatenate(
                [
                    jnp.where(
                        row8 < 4,
                        jnp.broadcast_to(v[c * 8 + 6 : c * 8 + 7], (8, 128)),
                        jnp.broadcast_to(v[c * 8 + 7 : c * 8 + 8], (8, 128)),
                    )
                    * mask2
                    for c in range(2)
                ],
                axis=0,
            )
        )
    spread = jnp.concatenate(split3(jnp.concatenate(spread, axis=1)), axis=0)
    factor = fold3(lax.dot_general(spread, weight2[...], NT, preferred_element_type=F32))
    total = buf2[0]
    for f in range(1, 8):
        total = total + buf2[f]
    update = jnp.concatenate(split3(total * factor), axis=0)
    for g in range(8):
        s = ys[(2, 1, 3, 0)[g // 2]] * 2 + cs[1 - g % 2]
        pair = jnp.concatenate([weight1[s], weight3[s]], axis=1)
        picked = fold3(lax.dot_general(update, pair, NN, preferred_element_type=F32))
        a = [picked[c * 8 : c * 8 + 8, 0:128] for c in range(2)]
        o = [jnp.where(owned[c], picked[c * 8 : c * 8 + 8, 128:256], 0.0) for c in range(2)]
        out = [jnp.where(first4, a[0], 0.0), jnp.where(first4, a[1], 0.0)]
        out.append(jnp.where(last2[0], a[0], 0.0) + jnp.where(last2[1], a[1], 0.0))
        out.append(o[0] + o[1])
        for k in range(4):
            src3[g * 4 + k : g * 4 + k + 1, :] = jnp.sum(out[k], axis=0, keepdims=True)
    for dev, _, _, g, _ in local_peers:
        send(2, src3.at[pl.ds(g * 4, 4), :], rows(buf3, mine), dev)
    own3, whole3 = settle(2, src3.at[pl.ds(28, 4), :], buf3, 4 * len(local_peers))
    own3.wait()
    whole3.wait_recv()
    part = [buf3[pl.ds(k, 64, stride=4), :] for k in range(4)]
    turned[0:128, :] = jnp.concatenate(part[0:2], axis=0).T
    rest = [
        jnp.where(front, part[2], pltpu.roll(part[3], 64, 1)),
        jnp.where(front, pltpu.roll(part[2], 64, 1), part[3]),
    ]
    turned[128:256, :] = jnp.concatenate(rest, axis=0).T
    for t in range(TILES):
        lhs = jnp.concatenate([turned[pl.ds(t * SLOTS + s, 8, stride=32), :] for s in range(SLOTS)], axis=1)
        lhs = jnp.concatenate(split3(lhs)[0:2], axis=0)
        got = lax.dot_general(lhs, halves[t], NN, preferred_element_type=F32)
        got = got[0:8] + got[8:16]
        got = got[:, 0:128] + got[:, 128:256]
        model_ref[:, t * 128 : (t + 1) * 128] = got[0:PN]
    for p in range(PN):
        upd_ref[p] = turned[192 + 4 * p : 196 + 4 * p, :]
    whole1.wait_send()
    whole2.wait_send()
    whole3.wait_send()


def local(kernels, basis, support_index, owner_order, precond, damping):
    hbm = pl.BlockSpec(memory_space=pltpu.HBM)
    vmem = pl.BlockSpec(memory_space=pltpu.VMEM)
    points = TILES * 128
    model, update = pl.pallas_call(
        kernel,
        out_shape=(
            pltpu.VMEM((PN, points), F32),
            pltpu.VMEM((PN, 4, 128), F32),
        ),
        in_specs=[hbm] * 6,
        out_specs=(vmem, vmem),
        scratch_shapes=[
            pltpu.VMEM((PN, 2, points), F32),
            pltpu.VMEM((TILES, SLOTS, 128, 128), F32),
            pltpu.VMEM((1, 128), jnp.int32),
            pltpu.VMEM((PN, 4, 128), F32),
            pltpu.SMEM((SLOTS, TILES), jnp.int32),
            pltpu.SMEM((PN,), F32),
            pltpu.VMEM((TILES, SLOTS * 128, 256), BF16),
            pltpu.VMEM((288, 128), F32),
            pltpu.VMEM((264, 128), F32),
            pltpu.VMEM((256, 128), F32),
            pltpu.VMEM((8, 16, 128), F32),
            pltpu.VMEM((32, 128), F32),
            pltpu.VMEM((264, 128), F32),
            pltpu.VMEM((288, 128), F32),
            pltpu.VMEM((8, 128, 128), BF16),
            pltpu.VMEM((8, 128, 128), BF16),
            pltpu.VMEM((8, 128, 128), BF16),
            pltpu.VMEM((128, 512), BF16),
            pltpu.VMEM((128, 128), F32),
            pltpu.SemaphoreType.DMA((5,)),
            pltpu.SemaphoreType.DMA((TILES,)),
            pltpu.SemaphoreType.DMA((3,)),
            pltpu.SemaphoreType.DMA((3,)),
            pltpu.SemaphoreType.DMA((3,)),
        ],
        compiler_params=pltpu.CompilerParams(
            collective_id=0, has_side_effects=True, vmem_limit_bytes=60 * 1024 * 1024
        ),
        cost_estimate=pl.CostEstimate(flops=10**9, bytes_accessed=2 * 10**6, transcendentals=0),
    )(
        kernels.transpose(1, 0, 2), basis, support_index.T, owner_order.reshape(1, 128),
        precond.transpose(1, 0, 2), damping,
    )
    return model, update.transpose(1, 0, 2)


def solution(mesh):
    in_specs = (
        P("event", None, "mesh"),
        P("mesh", None, None, None),
        P("mesh", None),
        P(),
        P("mesh", None, None),
        P(),
    )
    out_specs = (P(None, "mesh"), P("mesh", None, None))
    return jax.shard_map(local, mesh=mesh, in_specs=in_specs, out_specs=out_specs, check_vma=False)
```
